32 devices in a mesh: dp: 16 (over z, y, core), sub: 2 (over x).
Axes of the slice: x: 2, y: 2, z: 4, core: 2. Of those that a mesh axis runs over, the one named last changes fastest.
Arguments:
- activations: bfloat16 [64, 14, 14, 384], P(('dp', 'sub')), may hold values from -6 to 6
- cotangent: bfloat16 [64, 14, 14, 384], P(('dp', 'sub')), may hold values from -0.29882812 to 0.29882812
- kernel: bfloat16 [384, 1152], replicated, may hold values from -0.1875 to 0.1875
- channel_gain: float32 [384], replicated, may hold values from 0.5 to 4
- master_flat: float32 [442368], P(('dp', 'sub')), may hold values from -6 to 6
- moment_mean: float32 [442368], P(('dp', 'sub')), may hold values from -2.352 to 2.352
- moment_square: float32 [442368], P(('dp', 'sub')), may hold values from 0.0025088 to 0.06272
Outputs:
- input_grad: bfloat16 [64, 14, 14, 384], P(('dp', 'sub'))
- master_next: float32 [442368], P(('dp', 'sub'))
- mean_next: float32 [442368], P(('dp', 'sub'))
- square_next: float32 [442368], P(('dp', 'sub'))
- kernel_next: bfloat16 [384, 1152], replicated
The draws below stay inside these ranges and needn't reach their ends.
All inputs are finite; a program needn't handle non-finite values.
Results may differ from the reference program's by a relative error of at most 0.006.
Values may be sent and summed in bfloat16 or wider, within the bound.
A program may use at most 64 MiB of HBM per device.

```python
import math
import jax
import jax.numpy as jnp
from jax import lax

CMID = 384
CG = 128
SIDE = 14
IMG_DEV = 2
ADAM_STEP = 10
GROUPS = 3
FAN = 1152
IMAGES = 64


def draw_master_flat(key, part):
    subkeys = jax.random.split(jax.random.fold_in(key, 17), 3)
    row_scale = jnp.exp(jax.random.uniform(subkeys[0], (CMID, 1), jnp.float32, math.log(0.3), math.log(3.0)))
    col_scale = jnp.exp(jax.random.uniform(subkeys[1], (1, FAN), jnp.float32, math.log(0.3), math.log(3.0)))
    entries = jax.random.normal(subkeys[2], (CMID, FAN), jnp.float32)
    return jnp.clip(0.12 * row_scale * col_scale * entries, -6.0, 6.0).reshape(CMID * FAN)


def levels(key, extent, cuts, least, largest):
    level, own = 1.0, jax.random.fold_in(key, 6)
    for dim, blocks in cuts:
        heights = jnp.exp(jax.random.uniform(jax.random.fold_in(own, dim), (blocks,), jnp.float32, least / len(cuts), largest / len(cuts)))
        level = level * jnp.repeat(heights, extent[dim] // blocks).reshape([-1 if axis == dim else 1 for axis in range(len(extent))])
    return level


def centred(key, extent, spread, limit, shards=(), kind=jnp.bfloat16):
    result = jax.random.normal(key, extent, jnp.float32) * spread
    if len(shards) > 0:
        result = levels(key, extent, shards, -0.22, 0.18) * result
    return jnp.clip(result, min=-limit, max=limit).astype(kind)


def setup_inputs(seed: int = 0) -> dict:
    splits = jax.random.split(jax.random.key(seed), 8)
    return {
        "activations": centred(splits[0], (IMAGES, SIDE, SIDE, CMID), 1.0, 6.0, ((0, 32),)),
        "cotangent": centred(splits[1], (IMAGES, SIDE, SIDE, CMID), 0.05, 0.29882812, ((0, 32),)),
        "kernel": centred(splits[2], (CMID, FAN), FAN ** -0.5, 0.1875),
        "channel_gain": jnp.clip(jnp.exp(jax.random.uniform(splits[3], (CMID,), jnp.float32, math.log(0.5), math.log(4.0))), 0.5, 4.0),
        "master_flat": draw_master_flat(jax.random.fold_in(splits[7], 71), 0),
        "moment_mean": centred(splits[5], (CMID * FAN,), (0.0035 * (IMAGES * SIDE * SIDE) ** 0.5), 2.352, ((0, 32),), jnp.float32),
        "moment_square": jnp.clip(jnp.exp(math.log(0.06272) - 3.218876 * jax.random.uniform(splits[6], (CMID * FAN,), jnp.float32) ** levels(splits[6], (CMID * FAN,), ((0, 32),), -0.2, 0.2)), 0.0025088, 0.06272),
    }


HALF_ROOT = 0.7071067811865476
INV_ROOT_TAU = 0.3989422804014327

def gelu_slope(values):
    return 0.5 * (1.0 + lax.erf(values * HALF_ROOT)) + values * jnp.exp(-0.5 * values * values) * INV_ROOT_TAU

def forward(images, kernel_taps):
    batch, side = (images.shape[0], images.shape[1])
    padded = jnp.pad(images.astype(jnp.float32), ((0, 0), (1, 1), (1, 1), (0, 0))).reshape(batch, side + 2, side + 2, GROUPS, CG)
    total = jnp.zeros((batch, side, side, GROUPS, CG), jnp.float32)
    for tap_index in range(9):
        row_off, col_off = (tap_index // 3, tap_index % 3)
        window = padded[:, row_off:row_off + side, col_off:col_off + side]
        total = total + jnp.einsum('bhwgc,gdc->bhwgd', window, kernel_taps[:, :, tap_index, :])
    return total.reshape(batch, side, side, GROUPS * CG)

def input_back(pre_grad, kernel_taps):
    batch, side = (pre_grad.shape[0], pre_grad.shape[1])
    padded = jnp.pad(pre_grad.astype(jnp.float32), ((0, 0), (1, 1), (1, 1), (0, 0))).reshape(batch, side + 2, side + 2, GROUPS, CG)
    total = jnp.zeros((batch, side, side, GROUPS, CG), jnp.float32)
    for tap_index in range(9):
        row_off, col_off = (tap_index // 3, tap_index % 3)
        window = padded[:, 2 - row_off:2 - row_off + side, 2 - col_off:2 - col_off + side]
        total = total + jnp.einsum('bhwgd,gdc->bhwgc', window, kernel_taps[:, :, tap_index, :])
    return total.reshape(batch, side, side, GROUPS * CG)

def kernel_back(images, pre_grad):
    batch, side = (images.shape[0], images.shape[1])
    padded = jnp.pad(images.astype(jnp.float32), ((0, 0), (1, 1), (1, 1), (0, 0))).reshape(batch, side + 2, side + 2, GROUPS, CG)
    upstream = pre_grad.astype(jnp.float32).reshape(batch, side, side, GROUPS, CG)
    terms = []
    for tap_index in range(9):
        row_off, col_off = (tap_index // 3, tap_index % 3)
        window = padded[:, row_off:row_off + side, col_off:col_off + side]
        terms.append(jnp.einsum('bhwgc,bhwgd->gdc', window, upstream))
    return jnp.stack(terms, axis=2).reshape(GROUPS * CG, 9 * CG)

def reference(activations, cotangent, kernel, channel_gain, master_flat, moment_mean, moment_square):
    kernel_taps = kernel.astype(jnp.float32).reshape(GROUPS, CG, 9, CG)
    blocks = IMAGES // IMG_DEV
    image_blocks = activations.reshape(blocks, IMG_DEV, SIDE, SIDE, CMID)
    cot_blocks = cotangent.reshape(blocks, IMG_DEV, SIDE, SIDE, CMID)

    def scan_step(total, inputs_pair):
        images, upstream = inputs_pair
        preact = forward(images, kernel_taps)
        pre_grad = (upstream.astype(jnp.float32) * gelu_slope(preact)).astype(jnp.bfloat16)
        back = input_back(pre_grad, kernel_taps).astype(jnp.bfloat16)
        return (total + kernel_back(images, pre_grad), back)
    grad_full, back_blocks = lax.scan(scan_step, jnp.zeros((CMID, FAN), jnp.float32), (image_blocks, cot_blocks))
    input_grad = back_blocks.reshape(IMAGES, SIDE, SIDE, CMID)
    grad_full = grad_full.reshape(CMID * FAN)
    mean_next = 0.9 * moment_mean + 0.1 * grad_full
    square_next = 0.999 * moment_square + 0.001 * grad_full * grad_full
    fix_mean = 1.0 - 0.9 ** ADAM_STEP
    fix_square = 1.0 - 0.999 ** ADAM_STEP
    update = mean_next / fix_mean / (jnp.sqrt(square_next / fix_square) + 1e-08)
    master_next = master_flat - 0.02 * update
    matrix = master_next.reshape(CMID, FAN)
    chan_mean = lax.optimization_barrier(jnp.sum(matrix, axis=1)) / FAN
    chan_var = lax.optimization_barrier(jnp.sum(matrix * matrix, axis=1)) / FAN - chan_mean * chan_mean
    chan_scale = channel_gain / jnp.sqrt(FAN * chan_var + 0.0001)
    kernel_next = ((matrix - chan_mean[:, None]) * chan_scale[:, None]).astype(jnp.bfloat16)
    return (input_grad, master_next, mean_next, square_next, kernel_next)
```

```python
import jax
import jax.numpy as jnp
from jax import lax
from jax.experimental import pallas as pl
from jax.experimental.pallas import tpu as pltpu
from jax.sharding import PartitionSpec as P

CMID = 384
CG = 128
ADAM_STEP = 10
GROUPS = 3
FAN = 1152


HALF_ROOT = 0.7071067811865476
INV_ROOT_TAU = 0.3989422804014327


def gelu_slope(values):
    return (
        0.5 * (1.0 + lax.erf(values * HALF_ROOT))
        + values * jnp.exp(-0.5 * values * values) * INV_ROOT_TAU
    )


def forward(images, kernel_taps):
    batch, side = (images.shape[0], images.shape[1])
    padded = jnp.pad(images, ((0, 0), (1, 1), (1, 1), (0, 0))).reshape(
        batch, side + 2, side + 2, GROUPS, CG
    )
    total = jnp.zeros((batch, side, side, GROUPS, CG), jnp.float32)
    for tap_index in range(9):
        row_off, col_off = (tap_index // 3, tap_index % 3)
        window = padded[:, row_off : row_off + side, col_off : col_off + side]
        total = total + jnp.einsum(
            "bhwgc,gdc->bhwgd",
            window,
            kernel_taps[:, :, tap_index, :],
            preferred_element_type=jnp.float32,
        )
    return total.reshape(batch, side, side, GROUPS * CG)


def input_back(pre_grad, kernel_taps):
    batch, side = (pre_grad.shape[0], pre_grad.shape[1])
    padded = jnp.pad(pre_grad, ((0, 0), (1, 1), (1, 1), (0, 0))).reshape(
        batch, side + 2, side + 2, GROUPS, CG
    )
    total = jnp.zeros((batch, side, side, GROUPS, CG), jnp.float32)
    for tap_index in range(9):
        row_off, col_off = (tap_index // 3, tap_index % 3)
        window = padded[:, 2 - row_off : 2 - row_off + side, 2 - col_off : 2 - col_off + side]
        total = total + jnp.einsum(
            "bhwgd,gdc->bhwgc",
            window,
            kernel_taps[:, :, tap_index, :],
            preferred_element_type=jnp.float32,
        )
    return total.reshape(batch, side, side, GROUPS * CG)


def kernel_back(images, pre_grad):
    batch, side = (images.shape[0], images.shape[1])
    padded = jnp.pad(images, ((0, 0), (1, 1), (1, 1), (0, 0))).reshape(
        batch, side + 2, side + 2, GROUPS, CG
    )
    upstream = pre_grad.reshape(batch, side, side, GROUPS, CG)
    terms = []
    for tap_index in range(9):
        row_off, col_off = (tap_index // 3, tap_index % 3)
        window = padded[:, row_off : row_off + side, col_off : col_off + side]
        terms.append(
            jnp.einsum("bhwgc,bhwgd->gdc", window, upstream, preferred_element_type=jnp.float32)
        )
    return jnp.stack(terms, axis=2).reshape(GROUPS * CG * 9 * CG)


def channel_scale(sum_plain, sum_square, channel_gain):
    chan_mean = sum_plain / FAN
    chan_var = sum_square / FAN - chan_mean * chan_mean
    return (chan_mean, channel_gain / jnp.sqrt(FAN * chan_var + 0.0001))


def on_device(
    activations, cotangent, kernel, channel_gain, master_flat, moment_mean, moment_square
):
    kernel_taps = kernel.reshape(GROUPS, CG, 9, CG)
    preact = forward(activations, kernel_taps)
    pre_grad = (cotangent.astype(jnp.float32) * gelu_slope(preact)).astype(jnp.bfloat16)
    grad_full = kernel_back(activations, pre_grad)
    grad_shard = lax.psum_scatter(grad_full, ("dp", "sub"), scatter_dimension=0, tiled=True)
    input_grad = input_back(pre_grad, kernel_taps).astype(jnp.bfloat16)
    mean_next = 0.9 * moment_mean + 0.1 * grad_shard
    square_next = 0.999 * moment_square + 0.001 * grad_shard * grad_shard
    fix_mean = 1.0 - 0.9**ADAM_STEP
    fix_square = 1.0 - 0.999**ADAM_STEP
    update = mean_next / fix_mean / (jnp.sqrt(square_next / fix_square) + 1e-08)
    master_next = master_flat - 0.02 * update
    shard_len = master_next.shape[0]
    shard_start = lax.axis_index(("dp", "sub")) * shard_len
    first_chan = shard_start // FAN
    chan_span = shard_len // FAN + 2
    offsets = shard_start + jnp.arange(shard_len, dtype=jnp.int32)
    local_chan = offsets // FAN - first_chan
    onehot = (local_chan[:, None] == jnp.arange(chan_span, dtype=jnp.int32)[None, :]).astype(
        jnp.float32
    )
    highest = lax.Precision.HIGHEST
    plain_part = jnp.dot(master_next, onehot, precision=highest)
    square_part = jnp.dot(master_next * master_next, onehot, precision=highest)
    empty = jnp.zeros((CMID + chan_span,), jnp.float32)
    plain_full = lax.dynamic_update_slice(empty, plain_part, (first_chan,))[:CMID]
    square_full = lax.dynamic_update_slice(empty, square_part, (first_chan,))[:CMID]
    sum_plain, sum_square = lax.psum((plain_full, square_full), ("dp", "sub"))
    chan_mean, chan_scale = channel_scale(sum_plain, sum_square, channel_gain)
    mean_window = lax.dynamic_slice(
        jnp.concatenate([chan_mean, empty[:chan_span]]), (first_chan,), (chan_span,)
    )
    scale_window = lax.dynamic_slice(
        jnp.concatenate([chan_scale, empty[:chan_span]]), (first_chan,), (chan_span,)
    )
    entry_mean = jnp.dot(onehot, mean_window, precision=highest)
    entry_scale = jnp.dot(onehot, scale_window, precision=highest)
    standard_shard = ((master_next - entry_mean) * entry_scale).astype(jnp.bfloat16)
    kernel_next = lax.all_gather(standard_shard, ("dp", "sub"), axis=0, tiled=True).reshape(
        CMID, FAN
    )
    return (input_grad, master_next, mean_next, square_next, kernel_next)


MESH = pl.DeviceIdType.MESH
SHARD_ROWS = 12
LINES = SHARD_ROWS * 9
SLOT = 112
F32 = jnp.float32
BF16 = jnp.bfloat16


def step_kernel(
    act, cot, ker, gain, master, mean, square,
    back, master_out, mean_out, square_out, ker_out,
    pad32, cot32, xl, gl, gf, gb, r1, s1, r2, s2, r3, s3, r4, kb, kf, rows_in, rows_out,
    rs_send, rs_recv, ag_send, ag_recv,
):
    dp = lax.axis_index("dp")
    x = lax.axis_index("sub")
    z, y, c = lax.div(dp, 4), lax.rem(lax.div(dp, 2), 2), lax.rem(dp, 2)
    core_dev = (dp + 1 - 2 * c, x)
    x_dev = (dp, 1 - x)
    y_dev = (dp + 2 - 4 * y, x)

    def z_dev(other):
        return (other * 4 + lax.rem(dp, 4), x)

    def ahead(k):
        return lax.rem(z + k, 4)

    def behind(k):
        return lax.rem(z + 4 - k, 4)

    barrier = pltpu.get_barrier_semaphore()
    for device in (core_dev, x_dev, y_dev, z_dev(ahead(1)), z_dev(ahead(2)), z_dev(ahead(3))):
        pl.semaphore_signal(barrier, inc=1, device_id=device, device_id_type=MESH)

    pad32[:, :, 8:16, :] = jnp.zeros((2, 14, 8, CMID), F32)
    cot32[:, :, 8:16, :] = jnp.zeros((2, 14, 8, CMID), F32)
    pad32[:, :, 0:14, :] = act[...].astype(F32)
    cot32[:, :, 0:14, :] = cot[...].astype(F32)
    for edge in (0, 15):
        xl[:, edge] = jnp.zeros((2, 16, 9 * CG), BF16)
        gl[:, edge] = jnp.zeros((2, 16, 9 * CG), BF16)
    gf[3456:3472, :] = jnp.zeros((16, CG), F32)

    def shifted(values, by):
        return values if by == 0 else pltpu.roll(values, by % 448, 0)

    def grid(values):
        return values.astype(BF16).reshape(2, 14, 16, CG)

    def window(ref, top, g):
        return ref[:, top : top + 14, :, g * 384 : g * 384 + 384].reshape(448, 384)

    for g in range(GROUPS):
        chans = slice(g * CG, g * CG + CG)
        image = pad32[:, :, :, chans].reshape(448, CG)
        for kx in range(3):
            at = g * 384 + kx * CG
            xl[:, 1:15, :, at : at + CG] = grid(shifted(image, 1 - kx))
        preact = jnp.zeros((448, CG), F32)
        for ky in range(3):
            preact += lax.dot_general(
                window(xl, ky, g), ker[chans, ky * 384 : ky * 384 + 384],
                (((1,), (1,)), ((), ())), preferred_element_type=F32,
            )
        rounded = (cot32[:, :, :, chans].reshape(448, CG) * gelu_slope(preact)).astype(BF16)
        wide = rounded.astype(F32)
        for kx in range(3):
            at = g * 384 + kx * CG
            gl[:, 1:15, :, at : at + CG] = grid(shifted(wide, kx - 1))
        turned = wide.T.astype(BF16)
        for ky in range(3):
            part = jnp.dot(turned, window(xl, ky, g), preferred_element_type=F32)
            for kx in range(3):
                line = g * 9 * CG + ky * 3 + kx
                gf[pl.ds(line, CG, stride=9), :] = part[:, kx * CG : kx * CG + CG]

    for zc in range(4):
        for yc in range(2):
            for cc in range(2):
                for xc in range(2):
                    first = (((zc * 2 + yc) * 2 + cc) * 2 + xc) * LINES
                    gb[zc, cc, yc, xc] = gf[first : first + SLOT, :].astype(BF16)

    def input_back_group(g):
        chans = slice(g * CG, g * CG + CG)
        total = jnp.zeros((448, CG), F32)
        for ky in range(3):
            taps = [ker[chans, (ky * 3 + kx) * CG : (ky * 3 + kx) * CG + CG] for kx in range(3)]
            total += jnp.dot(
                window(gl, 2 - ky, g), jnp.concatenate(taps, axis=0), preferred_element_type=F32
            )
        back[:, :, :, chans] = total.reshape(2, 14, 16, CG)[:, :, 0:14, :].astype(BF16)

    def send(src, dst, send_sem, recv_sem, device):
        copy = pltpu.make_async_remote_copy(
            src_ref=src, dst_ref=dst, send_sem=send_sem, recv_sem=recv_sem,
            device_id=device, device_id_type=MESH,
        )
        copy.start()
        return copy

    def both(one, other):
        return one.astype(F32) + other.astype(F32)

    pl.semaphore_wait(barrier, 6)
    order = (2, 1, 3, 0)
    copies = {}
    for k in order:
        copies[1, k] = send(
            gb.at[ahead(k), 1 - c], r1.at[k], rs_send.at[0, k], rs_recv.at[0, k], core_dev
        )
    input_back_group(0)
    for k in order:
        copies[1, k].wait_recv()
        zc = ahead(k)
        for yc in range(2):
            for xc in range(2):
                one, two = (xc, yc) if k % 2 == 0 else (yc, xc)
                s1[k, one, two] = both(gb[zc, c, yc, xc], r1[k, yc, xc]).astype(BF16)
        mine, device = (x, x_dev) if k % 2 == 0 else (y, y_dev)
        copies[2, k] = send(
            s1.at[k, 1 - mine], r2.at[k], rs_send.at[1, k], rs_recv.at[1, k], device
        )
    input_back_group(1)
    for k in order:
        copies[2, k].wait_recv()
        one, two, device = (x, y, y_dev) if k % 2 == 0 else (y, x, x_dev)
        for b in range(2):
            s2[k, b] = both(s1[k, one, b], r2[k, b]).astype(BF16)
        copies[3, k] = send(
            s2.at[k, 1 - two], r3.at[k], rs_send.at[2, k], rs_recv.at[2, k], device
        )
    input_back_group(2)
    for k in order:
        copies[3, k].wait_recv()
        two = y if k % 2 == 0 else x
        if k != 0:
            s3[k] = both(s2[k, two], r3[k]).astype(BF16)
            copies[4, k] = send(
                s3.at[k], r4.at[k], rs_send.at[3, k], rs_recv.at[3, k], z_dev(ahead(k))
            )
    grad = both(s2[0, y], r3[0])
    for k in (1, 3, 2):
        copies[4, k].wait_recv()
        grad = grad + r4[k].astype(F32)
    grad = grad[0:LINES, :]

    mean_next = 0.9 * mean[...] + 0.1 * grad
    square_next = 0.999 * square[...] + 0.001 * grad * grad
    fix_mean = 1.0 - 0.9**ADAM_STEP
    fix_square = 1.0 - 0.999**ADAM_STEP
    update = mean_next / fix_mean / (jnp.sqrt(square_next / fix_square) + 1e-08)
    master_next = master[...] - 0.02 * update
    mean_out[...] = mean_next
    square_out[...] = square_next
    master_out[...] = master_next
    rows_in[0:LINES, :] = master_next
    taps = [rows_in[pl.ds(t, SHARD_ROWS, stride=9), :] for t in range(9)]
    plain, squares = taps[0], taps[0] * taps[0]
    for tap in taps[1:]:
        plain, squares = plain + tap, squares + tap * tap
    shape = (SHARD_ROWS, CMID)
    first_chan = (dp * 2 + x) * SHARD_ROWS
    own = lax.broadcasted_iota(jnp.int32, shape, 1) == (
        lax.broadcasted_iota(jnp.int32, shape, 0) + first_chan
    )
    own_gain = jnp.sum(jnp.where(own, gain[...], 0.0), axis=1, keepdims=True)
    chan_mean, chan_scale = channel_scale(
        jnp.sum(plain, axis=1, keepdims=True), jnp.sum(squares, axis=1, keepdims=True), own_gain
    )
    rows_out[104:SLOT, :] = jnp.zeros((8, CG), F32)
    for t in range(9):
        rows_out[pl.ds(t, SHARD_ROWS, stride=9), :] = (taps[t] - chan_mean) * chan_scale
    kb[z, c, y, x] = rows_out[...].astype(BF16)

    own_slot = kb.at[z, c, y, x]
    for k in (2, 1, 3):
        copies[5, k] = send(
            own_slot, own_slot, ag_send.at[0, k], ag_recv.at[0, k], z_dev(ahead(k))
        )
    order = (0, 1, 3, 2)
    for k in order:
        if k != 0:
            copies[5, k].wait_recv()
        slot = kb.at[behind(k), c, y, x]
        copies[6, k] = send(
            slot, slot, ag_send.at[1, k], ag_recv.at[1, k], x_dev if k % 2 == 0 else y_dev
        )
    for k in order:
        copies[6, k].wait_recv()
        zc = behind(k)
        slot = kb.at[zc, c, y] if k % 2 == 0 else kb.at[zc, c, :, x]
        copies[7, k] = send(
            slot, slot, ag_send.at[2, k], ag_recv.at[2, k], y_dev if k % 2 == 0 else x_dev
        )
    for k in order:
        copies[7, k].wait_recv()
        slot = kb.at[behind(k), c]
        copies[8, k] = send(slot, slot, ag_send.at[3, k], ag_recv.at[3, k], core_dev)
    for k in order:
        copies[8, k].wait_recv()
        zc = behind(k)
        for yc in range(2):
            for cc in range(2):
                for xc in range(2):
                    first = ((yc * 2 + cc) * 2 + xc) * LINES
                    kf[first : first + LINES, :] = kb[zc, cc, yc, xc].astype(F32)[0:LINES, :]
        rows = pl.ds(pl.multiple_of(zc * 96, 96), 96)
        for t in range(9):
            ker_out[rows, t * CG : t * CG + CG] = kf[pl.ds(t, 96, stride=9), :].astype(BF16)
    for copy in copies.values():
        copy.wait_send()


def fused_on_device(
    activations, cotangent, kernel, channel_gain, master_flat, moment_mean, moment_square
):
    vmem = pl.BlockSpec(memory_space=pltpu.VMEM)
    lines = jax.ShapeDtypeStruct((LINES, CG), F32)
    back, master_next, mean_next, square_next, kernel_next = pl.pallas_call(
        step_kernel,
        out_shape=(
            jax.ShapeDtypeStruct(activations.shape, BF16),
            lines,
            lines,
            lines,
            jax.ShapeDtypeStruct((CMID, FAN), BF16),
        ),
        in_specs=[vmem] * 7,
        out_specs=(vmem,) * 5,
        scratch_shapes=[
            pltpu.VMEM((2, 14, 16, CMID), F32),
            pltpu.VMEM((2, 14, 16, CMID), F32),
            pltpu.VMEM((2, 16, 16, 9 * CG), BF16),
            pltpu.VMEM((2, 16, 16, 9 * CG), BF16),
            pltpu.VMEM((3472, CG), F32),
            pltpu.VMEM((4, 2, 2, 2, SLOT, CG), BF16),
            pltpu.VMEM((4, 2, 2, SLOT, CG), BF16),
            pltpu.VMEM((4, 2, 2, SLOT, CG), BF16),
            pltpu.VMEM((4, 2, SLOT, CG), BF16),
            pltpu.VMEM((4, 2, SLOT, CG), BF16),
            pltpu.VMEM((4, SLOT, CG), BF16),
            pltpu.VMEM((4, SLOT, CG), BF16),
            pltpu.VMEM((4, SLOT, CG), BF16),
            pltpu.VMEM((4, 2, 2, 2, SLOT, CG), BF16),
            pltpu.VMEM((96 * 9, CG), F32),
            pltpu.VMEM((SLOT, CG), F32),
            pltpu.VMEM((SLOT, CG), F32),
            pltpu.SemaphoreType.DMA((4, 4)),
            pltpu.SemaphoreType.DMA((4, 4)),
            pltpu.SemaphoreType.DMA((4, 4)),
            pltpu.SemaphoreType.DMA((4, 4)),
        ],
        compiler_params=pltpu.CompilerParams(
            collective_id=0, has_side_effects=True, vmem_limit_bytes=40 * 1024 * 1024
        ),
        cost_estimate=pl.CostEstimate(
            flops=1_100_000_000, bytes_accessed=4_000_000, transcendentals=400_000
        ),
    )(
        activations, cotangent, kernel, channel_gain.reshape(1, CMID),
        master_flat.reshape(LINES, CG), moment_mean.reshape(LINES, CG),
        moment_square.reshape(LINES, CG),
    )
    return (
        back, master_next.reshape(-1), mean_next.reshape(-1), square_next.reshape(-1), kernel_next
    )


def solution(mesh):
    placed = (
        P(("dp", "sub"), None, None, None),
        P(("dp", "sub"), None, None, None),
        P(),
        P(),
        P(("dp", "sub")),
        P(("dp", "sub")),
        P(("dp", "sub")),
    )
    fused = dict(mesh.shape) == {"dp": 16, "sub": 2}
    return jax.shard_map(
        fused_on_device if fused else on_device,
        mesh=mesh,
        in_specs=placed,
        out_specs=(
            P(("dp", "sub"), None, None, None),
            P(("dp", "sub")),
            P(("dp", "sub")),
            P(("dp", "sub")),
            P(),
        ),
        check_vma=False,
    )
```

```python
import jax
import jax.numpy as jnp
from jax import lax
from jax.experimental import pallas as pl
from jax.experimental.pallas import tpu as pltpu
from jax.sharding import PartitionSpec as P

CMID = 384
CG = 128
ADAM_STEP = 10
GROUPS = 3
FAN = 1152


HALF_ROOT = 0.7071067811865476
INV_ROOT_TAU = 0.3989422804014327


def gelu_slope(values):
    return (
        0.5 * (1.0 + lax.erf(values * HALF_ROOT))
        + values * jnp.exp(-0.5 * values * values) * INV_ROOT_TAU
    )


def forward(images, kernel_taps):
    batch, side = (images.shape[0], images.shape[1])
    padded = jnp.pad(images, ((0, 0), (1, 1), (1, 1), (0, 0))).reshape(
        batch, side + 2, side + 2, GROUPS, CG
    )
    total = jnp.zeros((batch, side, side, GROUPS, CG), jnp.float32)
    for tap_index in range(9):
        row_off, col_off = (tap_index // 3, tap_index % 3)
        window = padded[:, row_off : row_off + side, col_off : col_off + side]
        total = total + jnp.einsum(
            "bhwgc,gdc->bhwgd",
            window,
            kernel_taps[:, :, tap_index, :],
            preferred_element_type=jnp.float32,
        )
    return total.reshape(batch, side, side, GROUPS * CG)


def input_back(pre_grad, kernel_taps):
    batch, side = (pre_grad.shape[0], pre_grad.shape[1])
    padded = jnp.pad(pre_grad, ((0, 0), (1, 1), (1, 1), (0, 0))).reshape(
        batch, side + 2, side + 2, GROUPS, CG
    )
    total = jnp.zeros((batch, side, side, GROUPS, CG), jnp.float32)
    for tap_index in range(9):
        row_off, col_off = (tap_index // 3, tap_index % 3)
        window = padded[:, 2 - row_off : 2 - row_off + side, 2 - col_off : 2 - col_off + side]
        total = total + jnp.einsum(
            "bhwgd,gdc->bhwgc",
            window,
            kernel_taps[:, :, tap_index, :],
            preferred_element_type=jnp.float32,
        )
    return total.reshape(batch, side, side, GROUPS * CG)


def kernel_back(images, pre_grad):
    batch, side = (images.shape[0], images.shape[1])
    padded = jnp.pad(images, ((0, 0), (1, 1), (1, 1), (0, 0))).reshape(
        batch, side + 2, side + 2, GROUPS, CG
    )
    upstream = pre_grad.reshape(batch, side, side, GROUPS, CG)
    terms = []
    for tap_index in range(9):
        row_off, col_off = (tap_index // 3, tap_index % 3)
        window = padded[:, row_off : row_off + side, col_off : col_off + side]
        terms.append(
            jnp.einsum("bhwgc,bhwgd->gdc", window, upstream, preferred_element_type=jnp.float32)
        )
    return jnp.stack(terms, axis=2).reshape(GROUPS * CG * 9 * CG)


def channel_scale(sum_plain, sum_square, channel_gain):
    chan_mean = sum_plain / FAN
    chan_var = sum_square / FAN - chan_mean * chan_mean
    return (chan_mean, channel_gain / jnp.sqrt(FAN * chan_var + 0.0001))


def on_device(
    activations, cotangent, kernel, channel_gain, master_flat, moment_mean, moment_square
):
    kernel_taps = kernel.reshape(GROUPS, CG, 9, CG)
    preact = forward(activations, kernel_taps)
    pre_grad = (cotangent.astype(jnp.float32) * gelu_slope(preact)).astype(jnp.bfloat16)
    grad_full = kernel_back(activations, pre_grad)
    grad_shard = lax.psum_scatter(grad_full, ("dp", "sub"), scatter_dimension=0, tiled=True)
    input_grad = input_back(pre_grad, kernel_taps).astype(jnp.bfloat16)
    mean_next = 0.9 * moment_mean + 0.1 * grad_shard
    square_next = 0.999 * moment_square + 0.001 * grad_shard * grad_shard
    fix_mean = 1.0 - 0.9**ADAM_STEP
    fix_square = 1.0 - 0.999**ADAM_STEP
    update = mean_next / fix_mean / (jnp.sqrt(square_next / fix_square) + 1e-08)
    master_next = master_flat - 0.02 * update
    shard_len = master_next.shape[0]
    shard_start = lax.axis_index(("dp", "sub")) * shard_len
    first_chan = shard_start // FAN
    chan_span = shard_len // FAN + 2
    offsets = shard_start + jnp.arange(shard_len, dtype=jnp.int32)
    local_chan = offsets // FAN - first_chan
    onehot = (local_chan[:, None] == jnp.arange(chan_span, dtype=jnp.int32)[None, :]).astype(
        jnp.float32
    )
    highest = lax.Precision.HIGHEST
    plain_part = jnp.dot(master_next, onehot, precision=highest)
    square_part = jnp.dot(master_next * master_next, onehot, precision=highest)
    empty = jnp.zeros((CMID + chan_span,), jnp.float32)
    plain_full = lax.dynamic_update_slice(empty, plain_part, (first_chan,))[:CMID]
    square_full = lax.dynamic_update_slice(empty, square_part, (first_chan,))[:CMID]
    sum_plain, sum_square = lax.psum((plain_full, square_full), ("dp", "sub"))
    chan_mean, chan_scale = channel_scale(sum_plain, sum_square, channel_gain)
    mean_window = lax.dynamic_slice(
        jnp.concatenate([chan_mean, empty[:chan_span]]), (first_chan,), (chan_span,)
    )
    scale_window = lax.dynamic_slice(
        jnp.concatenate([chan_scale, empty[:chan_span]]), (first_chan,), (chan_span,)
    )
    entry_mean = jnp.dot(onehot, mean_window, precision=highest)
    entry_scale = jnp.dot(onehot, scale_window, precision=highest)
    standard_shard = ((master_next - entry_mean) * entry_scale).astype(jnp.bfloat16)
    kernel_next = lax.all_gather(standard_shard, ("dp", "sub"), axis=0, tiled=True).reshape(
        CMID, FAN
    )
    return (input_grad, master_next, mean_next, square_next, kernel_next)


MESH = pl.DeviceIdType.MESH
SHARD_ROWS = 12
LINES = SHARD_ROWS * 9
SLOT = 112
F32 = jnp.float32
BF16 = jnp.bfloat16


def step_kernel(
    act, cot, ker, gain, master, mean, square,
    back, master_out, mean_out, square_out, ker_out,
    pad32, cot32, xl, gl, gf, gb, r1, s1, r2, s2, r3, s3, held, r4, kb, kf, rows_in, rows_out,
    rs_send, rs_recv, ag_send, ag_recv,
):
    dp = lax.axis_index("dp")
    x = lax.axis_index("sub")
    z, y, c = lax.div(dp, 4), lax.rem(lax.div(dp, 2), 2), lax.rem(dp, 2)
    core_dev = (dp + 1 - 2 * c, x)
    x_dev = (dp, 1 - x)
    y_dev = (dp + 2 - 4 * y, x)

    def z_dev(other):
        return (other * 4 + lax.rem(dp, 4), x)

    def ahead(k):
        return lax.rem(z + k, 4)

    def behind(k):
        return lax.rem(z + 4 - k, 4)

    barrier = pltpu.get_barrier_semaphore()
    for device in (core_dev, x_dev, y_dev, z_dev(ahead(1)), z_dev(ahead(2)), z_dev(ahead(3))):
        pl.semaphore_signal(barrier, inc=1, device_id=device, device_id_type=MESH)

    pad32[:, :, 8:16, :] = jnp.zeros((2, 14, 8, CMID), F32)
    cot32[:, :, 8:16, :] = jnp.zeros((2, 14, 8, CMID), F32)
    pad32[:, :, 0:14, :] = act[...].astype(F32)
    cot32[:, :, 0:14, :] = cot[...].astype(F32)
    for edge in (0, 15):
        xl[:, edge] = jnp.zeros((2, 16, 9 * CG), BF16)
        gl[:, edge] = jnp.zeros((2, 16, 9 * CG), BF16)
    gf[3456:3472, :] = jnp.zeros((16, CG), F32)

    def shifted(values, by):
        return values if by == 0 else pltpu.roll(values, by % 448, 0)

    def grid(values):
        return values.astype(BF16).reshape(2, 14, 16, CG)

    def window(ref, top, g):
        return ref[:, top : top + 14, :, g * 384 : g * 384 + 384].reshape(448, 384)

    def gradient_group(g):
        chans = slice(g * CG, g * CG + CG)
        image = pad32[:, :, :, chans].reshape(448, CG)
        for kx in range(3):
            at = g * 384 + kx * CG
            xl[:, 1:15, :, at : at + CG] = grid(shifted(image, 1 - kx))
        preact = jnp.zeros((448, CG), F32)
        for ky in range(3):
            preact += lax.dot_general(
                window(xl, ky, g), ker[chans, ky * 384 : ky * 384 + 384],
                (((1,), (1,)), ((), ())), preferred_element_type=F32,
            )
        rounded = (cot32[:, :, :, chans].reshape(448, CG) * gelu_slope(preact)).astype(BF16)
        wide = rounded.astype(F32)
        turned = wide.T.astype(BF16)
        for ky in range(3):
            part = jnp.dot(turned, window(xl, ky, g), preferred_element_type=F32)
            for kx in range(3):
                line = g * 9 * CG + ky * 3 + kx
                gf[pl.ds(line, CG, stride=9), :] = part[:, kx * CG : kx * CG + CG]
        for kx in range(3):
            at = g * 384 + kx * CG
            gl[:, 1:15, :, at : at + CG] = grid(shifted(wide, kx - 1))

    def input_back_group(g):
        chans = slice(g * CG, g * CG + CG)
        total = jnp.zeros((448, CG), F32)
        for ky in range(3):
            taps = [ker[chans, (ky * 3 + kx) * CG : (ky * 3 + kx) * CG + CG] for kx in range(3)]
            total += jnp.dot(
                window(gl, 2 - ky, g), jnp.concatenate(taps, axis=0), preferred_element_type=F32
            )
        back[:, :, :, chans] = total.reshape(2, 14, 16, CG)[:, :, 0:14, :].astype(BF16)

    def remote(src, dst, send_sem, recv_sem, device):
        return pltpu.make_async_remote_copy(
            src_ref=src, dst_ref=dst, send_sem=send_sem, recv_sem=recv_sem,
            device_id=device, device_id_type=MESH,
        )

    def send(*parts):
        copy = remote(*parts)
        copy.start()
        return copy

    def both(one, other):
        return one.astype(F32) + other.astype(F32)

    copies = {}

    def pair_stage(zc):
        for yc in range(2):
            for cc in range(2):
                for xc in range(2):
                    first = (((zc * 2 + yc) * 2 + cc) * 2 + xc) * LINES
                    gb[zc, cc, yc, xc] = gf[first : first + SLOT, :].astype(BF16)
        copies[1, zc] = send(
            gb.at[zc, 1 - c], r1.at[zc], rs_send.at[0, zc], rs_recv.at[0, zc], core_dev
        )

    def first_stage(zc):
        copies[1, zc].wait_recv()
        for yc in range(2):
            for xc in range(2):
                one, two = (xc, yc) if zc % 2 == 0 else (yc, xc)
                s1[zc, one, two] = both(gb[zc, c, yc, xc], r1[zc, yc, xc]).astype(BF16)
        mine, device = (x, x_dev) if zc % 2 == 0 else (y, y_dev)
        copies[2, zc] = send(
            s1.at[zc, 1 - mine], r2.at[zc], rs_send.at[1, zc], rs_recv.at[1, zc], device
        )

    def second_stage(zc):
        copies[2, zc].wait_recv()
        one, two, device = (x, y, y_dev) if zc % 2 == 0 else (y, x, x_dev)
        for b in range(2):
            s2[zc, b] = both(s1[zc, one, b], r2[zc, b]).astype(BF16)
        copies[3, zc] = send(
            s2.at[zc, 1 - two], r3.at[zc], rs_send.at[2, zc], rs_recv.at[2, zc], device
        )

    def line_copy(src_z, dst_z):
        return remote(
            s3.at[dst_z], r4.at[src_z], rs_send.at[3, dst_z], rs_recv.at[3, src_z], z_dev(dst_z)
        )

    def line_stage(zc):
        copies[3, zc].wait_recv()
        two = y if zc % 2 == 0 else x
        total = both(s2[zc, two], r3[zc])
        held[zc] = total
        s3[zc] = total.astype(BF16)

        @pl.when(z != zc)
        def _():
            line_copy(z, zc).start()

    gradient_group(0)
    pl.semaphore_wait(barrier, 6)
    pair_stage(0)
    gradient_group(1)
    pair_stage(1)
    first_stage(0)
    gradient_group(2)
    pair_stage(2)
    pair_stage(3)
    first_stage(1)
    second_stage(0)
    first_stage(2)
    first_stage(3)
    input_back_group(0)
    second_stage(1)
    line_stage(0)
    second_stage(2)
    second_stage(3)
    input_back_group(1)
    line_stage(1)
    line_stage(2)
    line_stage(3)
    grad = held[z]
    for k in (1, 3, 2):
        line_copy(ahead(k), ahead(k)).wait_recv()
        grad = grad + r4[ahead(k)].astype(F32)
    grad = grad[0:LINES, :]

    mean_next = 0.9 * mean[...] + 0.1 * grad
    square_next = 0.999 * square[...] + 0.001 * grad * grad
    fix_mean = 1.0 - 0.9**ADAM_STEP
    fix_square = 1.0 - 0.999**ADAM_STEP
    update = mean_next / fix_mean / (jnp.sqrt(square_next / fix_square) + 1e-08)
    master_next = master[...] - 0.02 * update
    mean_out[...] = mean_next
    square_out[...] = square_next
    master_out[...] = master_next
    rows_in[0:LINES, :] = master_next
    taps = [rows_in[pl.ds(t, SHARD_ROWS, stride=9), :] for t in range(9)]
    plain, squares = taps[0], taps[0] * taps[0]
    for tap in taps[1:]:
        plain, squares = plain + tap, squares + tap * tap
    shape = (SHARD_ROWS, CG)
    first_chan = (dp * 2 + x) * SHARD_ROWS
    chan = lax.broadcasted_iota(jnp.int32, shape, 0) + first_chan
    lane = lax.broadcasted_iota(jnp.int32, shape, 1)
    picked = jnp.zeros(shape, F32)
    for g in range(GROUPS):
        picked += jnp.where(lane + g * CG == chan, gain[g : g + 1, :], 0.0)
    own_gain = jnp.sum(picked, axis=1, keepdims=True)
    chan_mean, chan_scale = channel_scale(
        jnp.sum(plain, axis=1, keepdims=True), jnp.sum(squares, axis=1, keepdims=True), own_gain
    )
    rows_out[104:SLOT, :] = jnp.zeros((8, CG), F32)
    for t in range(9):
        rows_out[pl.ds(t, SHARD_ROWS, stride=9), :] = (taps[t] - chan_mean) * chan_scale
    kb[z, c, y, x] = rows_out[...].astype(BF16)

    own_slot = kb.at[z, c, y, x]
    for k in (2, 1, 3):
        copies[5, k] = send(
            own_slot, own_slot, ag_send.at[0, k], ag_recv.at[0, k], z_dev(ahead(k))
        )
    input_back_group(2)
    order = (0, 1, 3, 2)
    for k in order:
        if k != 0:
            copies[5, k].wait_recv()
        slot = kb.at[behind(k), c, y, x]
        copies[6, k] = send(
            slot, slot, ag_send.at[1, k], ag_recv.at[1, k], x_dev if k % 2 == 0 else y_dev
        )
    for k in order:
        copies[6, k].wait_recv()
        zc = behind(k)
        slot = kb.at[zc, c, y] if k % 2 == 0 else kb.at[zc, c, :, x]
        copies[7, k] = send(
            slot, slot, ag_send.at[2, k], ag_recv.at[2, k], y_dev if k % 2 == 0 else x_dev
        )
    for k in order:
        copies[7, k].wait_recv()
        slot = kb.at[behind(k), c]
        copies[8, k] = send(slot, slot, ag_send.at[3, k], ag_recv.at[3, k], core_dev)
    for k in order:
        copies[8, k].wait_recv()
        zc = behind(k)
        for yc in range(2):
            for cc in range(2):
                for xc in range(2):
                    first = ((yc * 2 + cc) * 2 + xc) * LINES
                    kf[first : first + LINES, :] = kb[zc, cc, yc, xc].astype(F32)[0:LINES, :]
        rows = pl.ds(pl.multiple_of(zc * 96, 96), 96)
        for t in range(9):
            ker_out[rows, t * CG : t * CG + CG] = kf[pl.ds(t, 96, stride=9), :].astype(BF16)
    for copy in copies.values():
        copy.wait_send()
    for k in range(1, 4):
        line_copy(z, ahead(k)).wait_send()


def copy_kernel(*refs):
    count = (len(refs) - 1) // 2
    sems = refs[-1]
    copies = [
        pltpu.make_async_copy(refs[i], refs[count + i], sems.at[i]) for i in range(count)
    ]
    for copy in copies:
        copy.start()
    for copy in copies:
        copy.wait()


def put_out(*results):
    place = pl.BlockSpec(memory_space=pl.ANY)
    return pl.pallas_call(
        copy_kernel,
        out_shape=tuple(jax.ShapeDtypeStruct(r.shape, r.dtype) for r in results),
        in_specs=[place] * len(results),
        out_specs=(place,) * len(results),
        scratch_shapes=[pltpu.SemaphoreType.DMA((len(results),))],
    )(*results)


def fused_on_device(
    activations, cotangent, kernel, channel_gain, master_flat, moment_mean, moment_square
):
    vmem = pl.BlockSpec(memory_space=pltpu.VMEM)
    lines = jax.ShapeDtypeStruct((LINES, CG), F32)
    back, master_next, mean_next, square_next, kernel_next = pl.pallas_call(
        step_kernel,
        out_shape=(
            jax.ShapeDtypeStruct(activations.shape, BF16),
            lines,
            lines,
            lines,
            jax.ShapeDtypeStruct((CMID, FAN), BF16),
        ),
        in_specs=[vmem] * 7,
        out_specs=(vmem,) * 5,
        scratch_shapes=[
            pltpu.VMEM((2, 14, 16, CMID), F32),
            pltpu.VMEM((2, 14, 16, CMID), F32),
            pltpu.VMEM((2, 16, 16, 9 * CG), BF16),
            pltpu.VMEM((2, 16, 16, 9 * CG), BF16),
            pltpu.VMEM((3472, CG), F32),
            pltpu.VMEM((4, 2, 2, 2, SLOT, CG), BF16),
            pltpu.VMEM((4, 2, 2, SLOT, CG), BF16),
            pltpu.VMEM((4, 2, 2, SLOT, CG), BF16),
            pltpu.VMEM((4, 2, SLOT, CG), BF16),
            pltpu.VMEM((4, 2, SLOT, CG), BF16),
            pltpu.VMEM((4, SLOT, CG), BF16),
            pltpu.VMEM((4, SLOT, CG), BF16),
            pltpu.VMEM((4, SLOT, CG), F32),
            pltpu.VMEM((4, SLOT, CG), BF16),
            pltpu.VMEM((4, 2, 2, 2, SLOT, CG), BF16),
            pltpu.VMEM((96 * 9, CG), F32),
            pltpu.VMEM((SLOT, CG), F32),
            pltpu.VMEM((SLOT, CG), F32),
            pltpu.SemaphoreType.DMA((4, 4)),
            pltpu.SemaphoreType.DMA((4, 4)),
            pltpu.SemaphoreType.DMA((4, 4)),
            pltpu.SemaphoreType.DMA((4, 4)),
        ],
        compiler_params=pltpu.CompilerParams(
            collective_id=0, has_side_effects=True, vmem_limit_bytes=40 * 1024 * 1024
        ),
        cost_estimate=pl.CostEstimate(
            flops=1_100_000_000, bytes_accessed=4_000_000, transcendentals=400_000
        ),
    )(
        activations, cotangent, kernel, channel_gain.reshape(GROUPS, CG),
        master_flat.reshape(LINES, CG), moment_mean.reshape(LINES, CG),
        moment_square.reshape(LINES, CG),
    )
    master_next, mean_next, square_next, kernel_next = put_out(
        master_next, mean_next, square_next, kernel_next
    )
    return (
        back, master_next.reshape(-1), mean_next.reshape(-1), square_next.reshape(-1), kernel_next
    )


def solution(mesh):
    placed = (
        P(("dp", "sub"), None, None, None),
        P(("dp", "sub"), None, None, None),
        P(),
        P(),
        P(("dp", "sub")),
        P(("dp", "sub")),
        P(("dp", "sub")),
    )
    fused = dict(mesh.shape) == {"dp": 16, "sub": 2}
    return jax.shard_map(
        fused_on_device if fused else on_device,
        mesh=mesh,
        in_specs=placed,
        out_specs=(
            P(("dp", "sub"), None, None, None),
            P(("dp", "sub")),
            P(("dp", "sub")),
            P(("dp", "sub")),
            P(),
        ),
        check_vma=False,
    )
```

```python
import jax
import jax.numpy as jnp
from jax import lax
from jax.experimental import pallas as pl
from jax.experimental.pallas import tpu as pltpu
from jax.sharding import PartitionSpec as P

CMID = 384
CG = 128
ADAM_STEP = 10
GROUPS = 3
FAN = 1152


HALF_ROOT = 0.7071067811865476
INV_ROOT_TAU = 0.3989422804014327


def gelu_slope(values):
    return (
        0.5 * (1.0 + lax.erf(values * HALF_ROOT))
        + values * jnp.exp(-0.5 * values * values) * INV_ROOT_TAU
    )


def forward(images, kernel_taps):
    batch, side = (images.shape[0], images.shape[1])
    padded = jnp.pad(images, ((0, 0), (1, 1), (1, 1), (0, 0))).reshape(
        batch, side + 2, side + 2, GROUPS, CG
    )
    total = jnp.zeros((batch, side, side, GROUPS, CG), jnp.float32)
    for tap_index in range(9):
        row_off, col_off = (tap_index // 3, tap_index % 3)
        window = padded[:, row_off : row_off + side, col_off : col_off + side]
        total = total + jnp.einsum(
            "bhwgc,gdc->bhwgd",
            window,
            kernel_taps[:, :, tap_index, :],
            preferred_element_type=jnp.float32,
        )
    return total.reshape(batch, side, side, GROUPS * CG)


def input_back(pre_grad, kernel_taps):
    batch, side = (pre_grad.shape[0], pre_grad.shape[1])
    padded = jnp.pad(pre_grad, ((0, 0), (1, 1), (1, 1), (0, 0))).reshape(
        batch, side + 2, side + 2, GROUPS, CG
    )
    total = jnp.zeros((batch, side, side, GROUPS, CG), jnp.float32)
    for tap_index in range(9):
        row_off, col_off = (tap_index // 3, tap_index % 3)
        window = padded[:, 2 - row_off : 2 - row_off + side, 2 - col_off : 2 - col_off + side]
        total = total + jnp.einsum(
            "bhwgd,gdc->bhwgc",
            window,
            kernel_taps[:, :, tap_index, :],
            preferred_element_type=jnp.float32,
        )
    return total.reshape(batch, side, side, GROUPS * CG)


def kernel_back(images, pre_grad):
    batch, side = (images.shape[0], images.shape[1])
    padded = jnp.pad(images, ((0, 0), (1, 1), (1, 1), (0, 0))).reshape(
        batch, side + 2, side + 2, GROUPS, CG
    )
    upstream = pre_grad.reshape(batch, side, side, GROUPS, CG)
    terms = []
    for tap_index in range(9):
        row_off, col_off = (tap_index // 3, tap_index % 3)
        window = padded[:, row_off : row_off + side, col_off : col_off + side]
        terms.append(
            jnp.einsum("bhwgc,bhwgd->gdc", window, upstream, preferred_element_type=jnp.float32)
        )
    return jnp.stack(terms, axis=2).reshape(GROUPS * CG * 9 * CG)


def channel_scale(sum_plain, sum_square, channel_gain):
    chan_mean = sum_plain / FAN
    chan_var = sum_square / FAN - chan_mean * chan_mean
    return (chan_mean, channel_gain / jnp.sqrt(FAN * chan_var + 0.0001))


def adam(grad, master, mean, square):
    mean_next = 0.9 * mean + 0.1 * grad
    square_next = 0.999 * square + 0.001 * grad * grad
    fix_mean = 1.0 - 0.9**ADAM_STEP
    fix_square = 1.0 - 0.999**ADAM_STEP
    update = mean_next / fix_mean / (jnp.sqrt(square_next / fix_square) + 1e-08)
    return (master - 0.02 * update, mean_next, square_next)


def on_device(
    activations, cotangent, kernel, channel_gain, master_flat, moment_mean, moment_square
):
    kernel_taps = kernel.reshape(GROUPS, CG, 9, CG)
    preact = forward(activations, kernel_taps)
    pre_grad = (cotangent.astype(jnp.float32) * gelu_slope(preact)).astype(jnp.bfloat16)
    grad_full = kernel_back(activations, pre_grad)
    grad_shard = lax.psum_scatter(grad_full, ("dp", "sub"), scatter_dimension=0, tiled=True)
    input_grad = input_back(pre_grad, kernel_taps).astype(jnp.bfloat16)
    master_next, mean_next, square_next = adam(
        grad_shard, master_flat, moment_mean, moment_square
    )
    shard_len = master_next.shape[0]
    shard_start = lax.axis_index(("dp", "sub")) * shard_len
    first_chan = shard_start // FAN
    chan_span = shard_len // FAN + 2
    offsets = shard_start + jnp.arange(shard_len, dtype=jnp.int32)
    local_chan = offsets // FAN - first_chan
    onehot = (local_chan[:, None] == jnp.arange(chan_span, dtype=jnp.int32)[None, :]).astype(
        jnp.float32
    )
    highest = lax.Precision.HIGHEST
    plain_part = jnp.dot(master_next, onehot, precision=highest)
    square_part = jnp.dot(master_next * master_next, onehot, precision=highest)
    empty = jnp.zeros((CMID + chan_span,), jnp.float32)
    plain_full = lax.dynamic_update_slice(empty, plain_part, (first_chan,))[:CMID]
    square_full = lax.dynamic_update_slice(empty, square_part, (first_chan,))[:CMID]
    sum_plain, sum_square = lax.psum((plain_full, square_full), ("dp", "sub"))
    chan_mean, chan_scale = channel_scale(sum_plain, sum_square, channel_gain)
    mean_window = lax.dynamic_slice(
        jnp.concatenate([chan_mean, empty[:chan_span]]), (first_chan,), (chan_span,)
    )
    scale_window = lax.dynamic_slice(
        jnp.concatenate([chan_scale, empty[:chan_span]]), (first_chan,), (chan_span,)
    )
    entry_mean = jnp.dot(onehot, mean_window, precision=highest)
    entry_scale = jnp.dot(onehot, scale_window, precision=highest)
    standard_shard = ((master_next - entry_mean) * entry_scale).astype(jnp.bfloat16)
    kernel_next = lax.all_gather(standard_shard, ("dp", "sub"), axis=0, tiled=True).reshape(
        CMID, FAN
    )
    return (input_grad, master_next, mean_next, square_next, kernel_next)


MESH = pl.DeviceIdType.MESH
SHARD_ROWS = 12
LINES = SHARD_ROWS * 9
SLOT = 112
F32 = jnp.float32
BF16 = jnp.bfloat16


def step_kernel(
    act, cot, ker, gain, master, mean, square,
    back, grad_out, ker_out,
    pad32, cot32, xl, gl, gf, gb, r1, s1, r2, s3, r4, kb, kf, rows_in, rows_out,
    rs_send, rs_recv, ag_send, ag_recv,
):
    dp = lax.axis_index("dp")
    x = lax.axis_index("sub")
    z, y, c = lax.div(dp, 4), lax.rem(lax.div(dp, 2), 2), lax.rem(dp, 2)
    core_dev = (dp + 1 - 2 * c, x)
    x_dev = (dp, 1 - x)
    y_dev = (dp + 2 - 4 * y, x)
    cross_dev = (dp + 2 - 4 * y, 1 - x)

    def z_dev(other):
        return (other * 4 + lax.rem(dp, 4), x)

    def ahead(k):
        return lax.rem(z + k, 4)

    def behind(k):
        return lax.rem(z + 4 - k, 4)

    barrier = pltpu.get_barrier_semaphore()
    plane = (x_dev, y_dev, cross_dev)
    line = tuple(z_dev(ahead(k)) for k in (1, 2, 3))
    for device in (core_dev, *plane, *line):
        pl.semaphore_signal(barrier, inc=1, device_id=device, device_id_type=MESH)

    for wide_ref, narrow in ((pad32, act), (cot32, cot)):
        wide_ref[:, 24:32, :] = jnp.zeros((14, 8, CMID), F32)
        wide_ref[:, 0:28, :] = narrow[...].astype(F32)
    for edge in (0, 15):
        xl[edge] = jnp.zeros((32, 9 * CG), BF16)
        gl[edge] = jnp.zeros((32, 9 * CG), BF16)
    gf[3456:3472, :] = jnp.zeros((16, CG), F32)

    def shifted(values, by):
        return values if by == 0 else pltpu.roll(values, (2 * by) % 448, 0)

    def grid(values):
        return values.astype(BF16).reshape(14, 32, CG)

    def window(ref, top, g):
        return ref[top : top + 14, :, g * 384 : g * 384 + 384].reshape(448, 384)

    def gradient_group(g):
        chans = slice(g * CG, g * CG + CG)
        image = pad32[:, :, chans].reshape(448, CG)
        for kx in range(3):
            at = g * 384 + kx * CG
            xl[1:15, :, at : at + CG] = grid(shifted(image, 1 - kx))
        preact = jnp.zeros((448, CG), F32)
        for ky in range(3):
            preact += lax.dot_general(
                window(xl, ky, g), ker[chans, ky * 384 : ky * 384 + 384],
                (((1,), (1,)), ((), ())), preferred_element_type=F32,
            )
        rounded = (cot32[:, :, chans].reshape(448, CG) * gelu_slope(preact)).astype(BF16)
        wide = rounded.astype(F32)
        turned = wide.T.astype(BF16)
        for ky in range(3):
            part = jnp.dot(turned, window(xl, ky, g), preferred_element_type=F32)
            for kx in range(3):
                line = g * 9 * CG + ky * 3 + kx
                gf[pl.ds(line, CG, stride=9), :] = part[:, kx * CG : kx * CG + CG]
        for kx in range(3):
            at = g * 384 + kx * CG
            gl[1:15, :, at : at + CG] = grid(shifted(wide, kx - 1))

    def input_back_group(g):
        chans = slice(g * CG, g * CG + CG)
        total = jnp.zeros((448, CG), F32)
        for ky in range(3):
            taps = [ker[chans, (ky * 3 + kx) * CG : (ky * 3 + kx) * CG + CG] for kx in range(3)]
            total += jnp.dot(
                window(gl, 2 - ky, g), jnp.concatenate(taps, axis=0), preferred_element_type=F32
            )
        back[:, :, chans] = total.reshape(14, 32, CG)[:, 0:28, :].astype(BF16)

    def remote(src, dst, send_sem, recv_sem, device):
        return pltpu.make_async_remote_copy(
            src_ref=src, dst_ref=dst, send_sem=send_sem, recv_sem=recv_sem,
            device_id=device, device_id_type=MESH,
        )

    def send(*parts):
        copy = remote(*parts)
        copy.start()
        return copy

    def both(one, other):
        return one.astype(F32) + other.astype(F32)

    copies = {}

    def pair_stage(zc):
        for yc in range(2):
            for cc in range(2):
                for xc in range(2):
                    first = (((zc * 2 + yc) * 2 + cc) * 2 + xc) * LINES
                    gb[zc, cc, yc, xc] = gf[first : first + SLOT, :].astype(BF16)
        copies[1, zc] = send(
            gb.at[zc, 1 - c], r1.at[zc], rs_send.at[0, zc], rs_recv.at[0, zc], core_dev
        )

    def plane_stage(k):
        zc = ahead(k)
        remote(
            gb.at[zc, 1 - c], r1.at[zc], rs_send.at[0, zc], rs_recv.at[0, zc], core_dev
        ).wait_recv()
        for yc in range(2):
            for xc in range(2):
                s1[k, yc, xc] = both(gb[zc, c, yc, xc], r1[zc, yc, xc]).astype(BF16)
        parts = (s1.at[k, y, 1 - x], s1.at[k, 1 - y, x], s1.at[k, 1 - y, 1 - x])
        for j in range(3):
            copies[2 + j, k] = send(
                parts[j], r2.at[k, j], rs_send.at[1 + j, k], rs_recv.at[1 + j, k], plane[j]
            )

    def plane_sum(k):
        total = s1[k, y, x].astype(F32)
        for j in range(3):
            copies[2 + j, k].wait_recv()
            total = total + r2[k, j].astype(F32)
        return total

    gradient_group(0)
    pl.semaphore_wait(barrier, 7)
    pair_stage(0)
    gradient_group(1)
    pair_stage(1)
    gradient_group(2)
    pair_stage(2)
    pair_stage(3)
    input_back_group(0)
    order = (2, 1, 3, 0)
    for k in order:
        plane_stage(k)
    input_back_group(1)
    for k in order[0:3]:
        s3[k] = plane_sum(k).astype(BF16)
        copies[5, k] = send(
            s3.at[k], r4.at[k], rs_send.at[4, k], rs_recv.at[4, k], line[k - 1]
        )
    grad = plane_sum(0)
    input_back_group(2)
    for k in (1, 3, 2):
        copies[5, k].wait_recv()
        grad = grad + r4[k].astype(F32)
    grad = grad[0:LINES, :]
    grad_out[...] = grad

    master_next, _, _ = adam(grad, master[...], mean[...], square[...])
    rows_in[0:LINES, :] = master_next
    taps = [rows_in[pl.ds(t, SHARD_ROWS, stride=9), :] for t in range(9)]
    plain, squares = taps[0], taps[0] * taps[0]
    for tap in taps[1:]:
        plain, squares = plain + tap, squares + tap * tap
    shape = (SHARD_ROWS, CG)
    first_chan = (dp * 2 + x) * SHARD_ROWS
    chan = lax.broadcasted_iota(jnp.int32, shape, 0) + first_chan
    lane = lax.broadcasted_iota(jnp.int32, shape, 1)
    picked = jnp.zeros(shape, F32)
    for g in range(GROUPS):
        picked += jnp.where(lane + g * CG == chan, gain[g : g + 1, :], 0.0)
    own_gain = jnp.sum(picked, axis=1, keepdims=True)
    chan_mean, chan_scale = channel_scale(
        jnp.sum(plain, axis=1, keepdims=True), jnp.sum(squares, axis=1, keepdims=True), own_gain
    )
    rows_out[104:SLOT, :] = jnp.zeros((8, CG), F32)
    for t in range(9):
        rows_out[pl.ds(t, SHARD_ROWS, stride=9), :] = (taps[t] - chan_mean) * chan_scale
    kb[z, c, y, x] = rows_out[...].astype(BF16)

    def spread(k, slot, step, device):
        copies[step, k] = send(
            slot, slot, ag_send.at[step - 6, k], ag_recv.at[step - 6, k], device
        )

    def spread_own(k):
        slot = kb.at[behind(k), c, y, x]
        if k != 0:
            copies[6, k].wait_recv()
        for j in range(3):
            spread(k, slot, 7 + j, plane[j])
        spread(k, slot, 10, core_dev)

    def relay(k):
        held = kb.at[behind(k), c]
        slots = (held.at[y, 1 - x], held.at[1 - y, x], held.at[1 - y, 1 - x])
        for j in range(3):
            copies[7 + j, k].wait_recv()
            spread(k, slots[j], 11 + j, core_dev)

    def finish(k):
        for step in range(10, 14):
            copies[step, k].wait_recv()
        zc = behind(k)
        for yc in range(2):
            for cc in range(2):
                for xc in range(2):
                    first = ((yc * 2 + cc) * 2 + xc) * LINES
                    kf[first : first + LINES, :] = kb[zc, cc, yc, xc].astype(F32)[0:LINES, :]
        rows = pl.ds(pl.multiple_of(zc * 96, 96), 96)
        for t in range(9):
            ker_out[rows, t * CG : t * CG + CG] = kf[pl.ds(t, 96, stride=9), :].astype(BF16)

    for k in (2, 1, 3):
        spread(k, kb.at[z, c, y, x], 6, line[k - 1])
    spread_own(0)
    spread_own(1)
    relay(0)
    spread_own(3)
    relay(1)
    spread_own(2)
    relay(3)
    finish(0)
    relay(2)
    finish(1)
    finish(3)
    finish(2)
    for copy in copies.values():
        copy.wait_send()


def fused_on_device(
    activations, cotangent, kernel, channel_gain, master_flat, moment_mean, moment_square
):
    side = activations.shape[1]

    def by_place(images):
        return jnp.transpose(images, (1, 2, 0, 3)).reshape(side, side * 2, CMID)

    vmem = pl.BlockSpec(memory_space=pltpu.VMEM)
    back, grad, kernel_next = pl.pallas_call(
        step_kernel,
        out_shape=(
            jax.ShapeDtypeStruct((side, side * 2, CMID), BF16),
            jax.ShapeDtypeStruct((LINES, CG), F32),
            jax.ShapeDtypeStruct((CMID, FAN), BF16),
        ),
        in_specs=[vmem] * 7,
        out_specs=(vmem,) * 3,
        scratch_shapes=[
            pltpu.VMEM((14, 32, CMID), F32),
            pltpu.VMEM((14, 32, CMID), F32),
            pltpu.VMEM((16, 32, 9 * CG), BF16),
            pltpu.VMEM((16, 32, 9 * CG), BF16),
            pltpu.VMEM((3472, CG), F32),
            pltpu.VMEM((4, 2, 2, 2, SLOT, CG), BF16),
            pltpu.VMEM((4, 2, 2, SLOT, CG), BF16),
            pltpu.VMEM((4, 2, 2, SLOT, CG), BF16),
            pltpu.VMEM((4, 3, SLOT, CG), BF16),
            pltpu.VMEM((4, SLOT, CG), BF16),
            pltpu.VMEM((4, SLOT, CG), BF16),
            pltpu.VMEM((4, 2, 2, 2, SLOT, CG), BF16),
            pltpu.VMEM((96 * 9, CG), F32),
            pltpu.VMEM((SLOT, CG), F32),
            pltpu.VMEM((SLOT, CG), F32),
            pltpu.SemaphoreType.DMA((5, 4)),
            pltpu.SemaphoreType.DMA((5, 4)),
            pltpu.SemaphoreType.DMA((8, 4)),
            pltpu.SemaphoreType.DMA((8, 4)),
        ],
        compiler_params=pltpu.CompilerParams(
            collective_id=0, has_side_effects=True, vmem_limit_bytes=40 * 1024 * 1024
        ),
        cost_estimate=pl.CostEstimate(
            flops=1_100_000_000, bytes_accessed=4_000_000, transcendentals=400_000
        ),
    )(
        by_place(activations), by_place(cotangent), kernel, channel_gain.reshape(GROUPS, CG),
        master_flat.reshape(LINES, CG), moment_mean.reshape(LINES, CG),
        moment_square.reshape(LINES, CG),
    )
    input_grad = jnp.transpose(back.reshape(side, side, 2, CMID), (2, 0, 1, 3))
    master_next, mean_next, square_next = adam(
        grad.reshape(-1), master_flat, moment_mean, moment_square
    )
    return (input_grad, master_next, mean_next, square_next, kernel_next)


def solution(mesh):
    placed = (
        P(("dp", "sub"), None, None, None),
        P(("dp", "sub"), None, None, None),
        P(),
        P(),
        P(("dp", "sub")),
        P(("dp", "sub")),
        P(("dp", "sub")),
    )
    fused = dict(mesh.shape) == {"dp": 16, "sub": 2}
    return jax.shard_map(
        fused_on_device if fused else on_device,
        mesh=mesh,
        in_specs=placed,
        out_specs=(
            P(("dp", "sub"), None, None, None),
            P(("dp", "sub")),
            P(("dp", "sub")),
            P(("dp", "sub")),
            P(),
        ),
        check_vma=False,
    )
```

```python
import jax
import jax.numpy as jnp
from jax import lax
from jax.experimental import pallas as pl
from jax.experimental.pallas import tpu as pltpu
from jax.sharding import PartitionSpec as P

CMID = 384
CG = 128
ADAM_STEP = 10
GROUPS = 3
FAN = 1152


HALF_ROOT = 0.7071067811865476
INV_ROOT_TAU = 0.3989422804014327


def gelu_slope(values):
    return (
        0.5 * (1.0 + lax.erf(values * HALF_ROOT))
        + values * jnp.exp(-0.5 * values * values) * INV_ROOT_TAU
    )


def forward(images, kernel_taps):
    batch, side = (images.shape[0], images.shape[1])
    padded = jnp.pad(images, ((0, 0), (1, 1), (1, 1), (0, 0))).reshape(
        batch, side + 2, side + 2, GROUPS, CG
    )
    total = jnp.zeros((batch, side, side, GROUPS, CG), jnp.float32)
    for tap_index in range(9):
        row_off, col_off = (tap_index // 3, tap_index % 3)
        window = padded[:, row_off : row_off + side, col_off : col_off + side]
        total = total + jnp.einsum(
            "bhwgc,gdc->bhwgd",
            window,
            kernel_taps[:, :, tap_index, :],
            preferred_element_type=jnp.float32,
        )
    return total.reshape(batch, side, side, GROUPS * CG)


def input_back(pre_grad, kernel_taps):
    batch, side = (pre_grad.shape[0], pre_grad.shape[1])
    padded = jnp.pad(pre_grad, ((0, 0), (1, 1), (1, 1), (0, 0))).reshape(
        batch, side + 2, side + 2, GROUPS, CG
    )
    total = jnp.zeros((batch, side, side, GROUPS, CG), jnp.float32)
    for tap_index in range(9):
        row_off, col_off = (tap_index // 3, tap_index % 3)
        window = padded[:, 2 - row_off : 2 - row_off + side, 2 - col_off : 2 - col_off + side]
        total = total + jnp.einsum(
            "bhwgd,gdc->bhwgc",
            window,
            kernel_taps[:, :, tap_index, :],
            preferred_element_type=jnp.float32,
        )
    return total.reshape(batch, side, side, GROUPS * CG)


def kernel_back(images, pre_grad):
    batch, side = (images.shape[0], images.shape[1])
    padded = jnp.pad(images, ((0, 0), (1, 1), (1, 1), (0, 0))).reshape(
        batch, side + 2, side + 2, GROUPS, CG
    )
    upstream = pre_grad.reshape(batch, side, side, GROUPS, CG)
    terms = []
    for tap_index in range(9):
        row_off, col_off = (tap_index // 3, tap_index % 3)
        window = padded[:, row_off : row_off + side, col_off : col_off + side]
        terms.append(
            jnp.einsum("bhwgc,bhwgd->gdc", window, upstream, preferred_element_type=jnp.float32)
        )
    return jnp.stack(terms, axis=2).reshape(GROUPS * CG * 9 * CG)


def channel_scale(sum_plain, sum_square, channel_gain):
    chan_mean = sum_plain / FAN
    chan_var = sum_square / FAN - chan_mean * chan_mean
    return (chan_mean, channel_gain / jnp.sqrt(FAN * chan_var + 0.0001))


def adam(grad, master, mean, square):
    mean_next = 0.9 * mean + 0.1 * grad
    square_next = 0.999 * square + 0.001 * grad * grad
    fix_mean = 1.0 - 0.9**ADAM_STEP
    fix_square = 1.0 - 0.999**ADAM_STEP
    update = mean_next / fix_mean / (jnp.sqrt(square_next / fix_square) + 1e-08)
    return (master - 0.02 * update, mean_next, square_next)


def on_device(
    activations, cotangent, kernel, channel_gain, master_flat, moment_mean, moment_square
):
    kernel_taps = kernel.reshape(GROUPS, CG, 9, CG)
    preact = forward(activations, kernel_taps)
    pre_grad = (cotangent.astype(jnp.float32) * gelu_slope(preact)).astype(jnp.bfloat16)
    grad_full = kernel_back(activations, pre_grad)
    grad_shard = lax.psum_scatter(grad_full, ("dp", "sub"), scatter_dimension=0, tiled=True)
    input_grad = input_back(pre_grad, kernel_taps).astype(jnp.bfloat16)
    master_next, mean_next, square_next = adam(
        grad_shard, master_flat, moment_mean, moment_square
    )
    shard_len = master_next.shape[0]
    shard_start = lax.axis_index(("dp", "sub")) * shard_len
    first_chan = shard_start // FAN
    chan_span = shard_len // FAN + 2
    offsets = shard_start + jnp.arange(shard_len, dtype=jnp.int32)
    local_chan = offsets // FAN - first_chan
    onehot = (local_chan[:, None] == jnp.arange(chan_span, dtype=jnp.int32)[None, :]).astype(
        jnp.float32
    )
    highest = lax.Precision.HIGHEST
    plain_part = jnp.dot(master_next, onehot, precision=highest)
    square_part = jnp.dot(master_next * master_next, onehot, precision=highest)
    empty = jnp.zeros((CMID + chan_span,), jnp.float32)
    plain_full = lax.dynamic_update_slice(empty, plain_part, (first_chan,))[:CMID]
    square_full = lax.dynamic_update_slice(empty, square_part, (first_chan,))[:CMID]
    sum_plain, sum_square = lax.psum((plain_full, square_full), ("dp", "sub"))
    chan_mean, chan_scale = channel_scale(sum_plain, sum_square, channel_gain)
    mean_window = lax.dynamic_slice(
        jnp.concatenate([chan_mean, empty[:chan_span]]), (first_chan,), (chan_span,)
    )
    scale_window = lax.dynamic_slice(
        jnp.concatenate([chan_scale, empty[:chan_span]]), (first_chan,), (chan_span,)
    )
    entry_mean = jnp.dot(onehot, mean_window, precision=highest)
    entry_scale = jnp.dot(onehot, scale_window, precision=highest)
    standard_shard = ((master_next - entry_mean) * entry_scale).astype(jnp.bfloat16)
    kernel_next = lax.all_gather(standard_shard, ("dp", "sub"), axis=0, tiled=True).reshape(
        CMID, FAN
    )
    return (input_grad, master_next, mean_next, square_next, kernel_next)


MESH = pl.DeviceIdType.MESH
SHARD_ROWS = 12
LINES = SHARD_ROWS * 9
SLOT = 112
F32 = jnp.float32
BF16 = jnp.bfloat16


def step_kernel(
    act, cot, ker, gain, master, mean, square,
    back, grad_out, ker_out,
    pad32, cot32, pre, xl, gl, gf, gb, r1, s1, r2, s2, r3, s3, r4, kb, kf, rows_in, rows_out,
    rs_send, rs_recv, ag_send, ag_recv,
):
    dp = lax.axis_index("dp")
    x = lax.axis_index("sub")
    z, y, c = lax.div(dp, 4), lax.rem(lax.div(dp, 2), 2), lax.rem(dp, 2)
    core_dev = (dp + 1 - 2 * c, x)
    x_dev = (dp, 1 - x)
    y_dev = (dp + 2 - 4 * y, x)

    def z_dev(other):
        return (other * 4 + lax.rem(dp, 4), x)

    z_high, z_low = lax.div(z, 2), lax.rem(z, 2)

    def partner(k):
        high = 1 - z_high if k >= 2 else z_high
        low = 1 - z_low if k % 2 == 1 else z_low
        return 2 * high + low

    barrier = pltpu.get_barrier_semaphore()
    line = tuple(z_dev(partner(k)) for k in range(4))
    for device in (core_dev, x_dev, y_dev, *line[1:]):
        pl.semaphore_signal(barrier, inc=1, device_id=device, device_id_type=MESH)

    for wide_ref, narrow in ((pad32, act), (cot32, cot)):
        wide_ref[:, 24:32, :] = jnp.zeros((14, 8, CMID), F32)
        wide_ref[:, 0:28, :] = narrow[...].astype(F32)
    for edge in (0, 15):
        xl[edge] = jnp.zeros((32, 9 * CG), BF16)
        gl[edge] = jnp.zeros((32, 9 * CG), BF16)
    gf[3456:3472, :] = jnp.zeros((16, CG), F32)

    def shifted(values, by):
        return values if by == 0 else pltpu.roll(values, (2 * by) % 448, 0)

    def grid(values):
        return values.astype(BF16).reshape(14, 32, CG)

    def window(ref, top, g):
        return ref[top : top + 14, :, g * 384 : g * 384 + 384].reshape(448, 384)

    def forward_group(g):
        chans = slice(g * CG, g * CG + CG)
        image = pad32[:, :, chans].reshape(448, CG)
        for kx in range(3):
            at = g * 384 + kx * CG
            xl[1:15, :, at : at + CG] = grid(shifted(image, 1 - kx))
        preact = jnp.zeros((448, CG), F32)
        for ky in range(3):
            preact += lax.dot_general(
                window(xl, ky, g), ker[chans, ky * 384 : ky * 384 + 384],
                (((1,), (1,)), ((), ())), preferred_element_type=F32,
            )
        pre[g] = preact

    def gradient_group(g):
        chans = slice(g * CG, g * CG + CG)
        rounded = (cot32[:, :, chans].reshape(448, CG) * gelu_slope(pre[g])).astype(BF16)
        wide = rounded.astype(F32)
        turned = wide.T.astype(BF16)
        for ky in range(3):
            part = jnp.dot(turned, window(xl, ky, g), preferred_element_type=F32)
            for kx in range(3):
                at = g * 9 * CG + ky * 3 + kx
                gf[pl.ds(at, CG, stride=9), :] = part[:, kx * CG : kx * CG + CG]
        for kx in range(3):
            at = g * 384 + kx * CG
            gl[1:15, :, at : at + CG] = grid(shifted(wide, kx - 1))

    def input_back_group(g):
        chans = slice(g * CG, g * CG + CG)
        total = jnp.zeros((448, CG), F32)
        for ky in range(3):
            taps = [ker[chans, (ky * 3 + kx) * CG : (ky * 3 + kx) * CG + CG] for kx in range(3)]
            total += jnp.dot(
                window(gl, 2 - ky, g), jnp.concatenate(taps, axis=0), preferred_element_type=F32
            )
        back[:, :, chans] = total.reshape(14, 32, CG)[:, 0:28, :].astype(BF16)

    def remote(src, dst, send_sem, recv_sem, device):
        return pltpu.make_async_remote_copy(
            src_ref=src, dst_ref=dst, send_sem=send_sem, recv_sem=recv_sem,
            device_id=device, device_id_type=MESH,
        )

    def send(*parts):
        copy = remote(*parts)
        copy.start()
        return copy

    def both(one, other):
        return one.astype(F32) + other.astype(F32)

    copies = {}

    def first_stage(k):
        copies[1, k].wait_recv()
        zc = partner(k)
        for yc in range(2):
            for xc in range(2):
                one, two = (xc, yc) if k % 2 == 0 else (yc, xc)
                s1[k, one, two] = both(gb[zc, c, yc, xc], r1[k, yc, xc]).astype(BF16)
        mine, device = (x, x_dev) if k % 2 == 0 else (y, y_dev)
        copies[2, k] = send(
            s1.at[k, 1 - mine], r2.at[k], rs_send.at[1, k], rs_recv.at[1, k], device
        )

    def second_stage(k):
        copies[2, k].wait_recv()
        one, two, device = (x, y, y_dev) if k % 2 == 0 else (y, x, x_dev)
        for b in range(2):
            s2[k, b] = both(s1[k, one, b], r2[k, b]).astype(BF16)
        copies[3, k] = send(
            s2.at[k, 1 - two], r3.at[k], rs_send.at[2, k], rs_recv.at[2, k], device
        )

    def plane_sum(k):
        copies[3, k].wait_recv()
        return both(s2[k, y if k % 2 == 0 else x], r3[k])

    forward_group(0)
    forward_group(1)
    gradient_group(0)
    forward_group(2)
    gradient_group(1)
    gradient_group(2)
    for zc in range(4):
        for yc in range(2):
            for cc in range(2):
                for xc in range(2):
                    first = (((zc * 2 + yc) * 2 + cc) * 2 + xc) * LINES
                    gb[zc, cc, yc, xc] = gf[first : first + SLOT, :].astype(BF16)
    pl.semaphore_wait(barrier, 6)
    order = (3, 2, 1, 0)
    for k in order:
        copies[1, k] = send(
            gb.at[partner(k), 1 - c], r1.at[k], rs_send.at[0, k], rs_recv.at[0, k], core_dev
        )
    input_back_group(0)
    for k in order:
        first_stage(k)
    input_back_group(1)
    for k in order:
        second_stage(k)
    input_back_group(2)
    for k in (3, 2, 1):
        s3[k] = plane_sum(k).astype(BF16)
        copies[4, k] = send(s3.at[k], r4.at[k], rs_send.at[3, k], rs_recv.at[3, k], line[k])
    grad = plane_sum(0)
    for k in (1, 2, 3):
        copies[4, k].wait_recv()
        grad = grad + r4[k].astype(F32)
    grad = grad[0:LINES, :]
    grad_out[...] = grad

    master_next, _, _ = adam(grad, master[...], mean[...], square[...])
    rows_in[0:LINES, :] = master_next
    taps = [rows_in[pl.ds(t, SHARD_ROWS, stride=9), :] for t in range(9)]
    plain, squares = taps[0], taps[0] * taps[0]
    for tap in taps[1:]:
        plain, squares = plain + tap, squares + tap * tap
    shape = (SHARD_ROWS, CG)
    first_chan = (dp * 2 + x) * SHARD_ROWS
    chan = lax.broadcasted_iota(jnp.int32, shape, 0) + first_chan
    lane = lax.broadcasted_iota(jnp.int32, shape, 1)
    picked = jnp.zeros(shape, F32)
    for g in range(GROUPS):
        picked += jnp.where(lane + g * CG == chan, gain[g : g + 1, :], 0.0)
    own_gain = jnp.sum(picked, axis=1, keepdims=True)
    chan_mean, chan_scale = channel_scale(
        jnp.sum(plain, axis=1, keepdims=True), jnp.sum(squares, axis=1, keepdims=True), own_gain
    )
    rows_out[104:SLOT, :] = jnp.zeros((8, CG), F32)
    for t in range(9):
        rows_out[pl.ds(t, SHARD_ROWS, stride=9), :] = (taps[t] - chan_mean) * chan_scale
    kb[z, c, y, x] = rows_out[...].astype(BF16)

    def spread(k, step, slot, device):
        copies[step, k] = send(
            slot, slot, ag_send.at[step - 5, k], ag_recv.at[step - 5, k], device
        )

    def spread_own(k):
        if k != 0:
            copies[5, k].wait_recv()
        spread(k, 6, kb.at[partner(k), c, y, x], x_dev if k % 2 == 0 else y_dev)

    def spread_two(k):
        copies[6, k].wait_recv()
        held = kb.at[partner(k), c]
        if k % 2 == 0:
            spread(k, 7, held.at[y], y_dev)
        else:
            spread(k, 7, held.at[:, x], x_dev)

    def spread_four(k):
        copies[7, k].wait_recv()
        spread(k, 8, kb.at[partner(k), c], core_dev)

    def finish(k):
        copies[8, k].wait_recv()
        zc = partner(k)
        for yc in range(2):
            for cc in range(2):
                for xc in range(2):
                    first = ((yc * 2 + cc) * 2 + xc) * LINES
                    kf[first : first + LINES, :] = kb[zc, cc, yc, xc].astype(F32)[0:LINES, :]
        rows = pl.ds(pl.multiple_of(zc * 96, 96), 96)
        for t in range(9):
            ker_out[rows, t * CG : t * CG + CG] = kf[pl.ds(t, 96, stride=9), :].astype(BF16)

    for k in (3, 2, 1):
        spread(k, 5, kb.at[z, c, y, x], line[k])
    spread_own(0)
    spread_own(1)
    spread_two(0)
    spread_own(2)
    spread_two(1)
    spread_four(0)
    spread_own(3)
    spread_two(2)
    spread_four(1)
    finish(0)
    spread_two(3)
    spread_four(2)
    finish(1)
    spread_four(3)
    finish(2)
    finish(3)
    for copy in copies.values():
        copy.wait_send()


def fused_on_device(
    activations, cotangent, kernel, channel_gain, master_flat, moment_mean, moment_square
):
    side = activations.shape[1]

    def by_place(images):
        return jnp.transpose(images, (1, 2, 0, 3)).reshape(side, side * 2, CMID)

    vmem = pl.BlockSpec(memory_space=pltpu.VMEM)
    back, grad, kernel_next = pl.pallas_call(
        step_kernel,
        out_shape=(
            jax.ShapeDtypeStruct((side, side * 2, CMID), BF16),
            jax.ShapeDtypeStruct((LINES, CG), F32),
            jax.ShapeDtypeStruct((CMID, FAN), BF16),
        ),
        in_specs=[vmem] * 7,
        out_specs=(vmem,) * 3,
        scratch_shapes=[
            pltpu.VMEM((14, 32, CMID), F32),
            pltpu.VMEM((14, 32, CMID), F32),
            pltpu.VMEM((GROUPS, 448, CG), F32),
            pltpu.VMEM((16, 32, 9 * CG), BF16),
            pltpu.VMEM((16, 32, 9 * CG), BF16),
            pltpu.VMEM((3472, CG), F32),
            pltpu.VMEM((4, 2, 2, 2, SLOT, CG), BF16),
            pltpu.VMEM((4, 2, 2, SLOT, CG), BF16),
            pltpu.VMEM((4, 2, 2, SLOT, CG), BF16),
            pltpu.VMEM((4, 2, SLOT, CG), BF16),
            pltpu.VMEM((4, 2, SLOT, CG), BF16),
            pltpu.VMEM((4, SLOT, CG), BF16),
            pltpu.VMEM((4, SLOT, CG), BF16),
            pltpu.VMEM((4, SLOT, CG), BF16),
            pltpu.VMEM((4, 2, 2, 2, SLOT, CG), BF16),
            pltpu.VMEM((96 * 9, CG), F32),
            pltpu.VMEM((SLOT, CG), F32),
            pltpu.VMEM((SLOT, CG), F32),
            pltpu.SemaphoreType.DMA((4, 4)),
            pltpu.SemaphoreType.DMA((4, 4)),
            pltpu.SemaphoreType.DMA((4, 4)),
            pltpu.SemaphoreType.DMA((4, 4)),
        ],
        compiler_params=pltpu.CompilerParams(
            collective_id=0, has_side_effects=True, vmem_limit_bytes=40 * 1024 * 1024
        ),
        cost_estimate=pl.CostEstimate(
            flops=1_100_000_000, bytes_accessed=4_000_000, transcendentals=400_000
        ),
    )(
        by_place(activations), by_place(cotangent), kernel, channel_gain.reshape(GROUPS, CG),
        master_flat.reshape(LINES, CG), moment_mean.reshape(LINES, CG),
        moment_square.reshape(LINES, CG),
    )
    input_grad = jnp.transpose(back.reshape(side, side, 2, CMID), (2, 0, 1, 3))
    master_next, mean_next, square_next = adam(
        grad.reshape(-1), master_flat, moment_mean, moment_square
    )
    return (input_grad, master_next, mean_next, square_next, kernel_next)


def solution(mesh):
    placed = (
        P(("dp", "sub"), None, None, None),
        P(("dp", "sub"), None, None, None),
        P(),
        P(),
        P(("dp", "sub")),
        P(("dp", "sub")),
        P(("dp", "sub")),
    )
    fused = dict(mesh.shape) == {"dp": 16, "sub": 2}
    return jax.shard_map(
        fused_on_device if fused else on_device,
        mesh=mesh,
        in_specs=placed,
        out_specs=(
            P(("dp", "sub"), None, None, None),
            P(("dp", "sub")),
            P(("dp", "sub")),
            P(("dp", "sub")),
            P(),
        ),
        check_vma=False,
    )
```

```python
import jax
import jax.numpy as jnp
from jax import lax
from jax.experimental import pallas as pl
from jax.experimental.pallas import tpu as pltpu
from jax.sharding import PartitionSpec as P

CMID = 384
CG = 128
ADAM_STEP = 10
GROUPS = 3
FAN = 1152


HALF_ROOT = 0.7071067811865476
INV_ROOT_TAU = 0.3989422804014327


def gelu_slope(values):
    return (
        0.5 * (1.0 + lax.erf(values * HALF_ROOT))
        + values * jnp.exp(-0.5 * values * values) * INV_ROOT_TAU
    )


def forward(images, kernel_taps):
    batch, side = (images.shape[0], images.shape[1])
    padded = jnp.pad(images, ((0, 0), (1, 1), (1, 1), (0, 0))).reshape(
        batch, side + 2, side + 2, GROUPS, CG
    )
    total = jnp.zeros((batch, side, side, GROUPS, CG), jnp.float32)
    for tap_index in range(9):
        row_off, col_off = (tap_index // 3, tap_index % 3)
        window = padded[:, row_off : row_off + side, col_off : col_off + side]
        total = total + jnp.einsum(
            "bhwgc,gdc->bhwgd",
            window,
            kernel_taps[:, :, tap_index, :],
            preferred_element_type=jnp.float32,
        )
    return total.reshape(batch, side, side, GROUPS * CG)


def input_back(pre_grad, kernel_taps):
    batch, side = (pre_grad.shape[0], pre_grad.shape[1])
    padded = jnp.pad(pre_grad, ((0, 0), (1, 1), (1, 1), (0, 0))).reshape(
        batch, side + 2, side + 2, GROUPS, CG
    )
    total = jnp.zeros((batch, side, side, GROUPS, CG), jnp.float32)
    for tap_index in range(9):
        row_off, col_off = (tap_index // 3, tap_index % 3)
        window = padded[:, 2 - row_off : 2 - row_off + side, 2 - col_off : 2 - col_off + side]
        total = total + jnp.einsum(
            "bhwgd,gdc->bhwgc",
            window,
            kernel_taps[:, :, tap_index, :],
            preferred_element_type=jnp.float32,
        )
    return total.reshape(batch, side, side, GROUPS * CG)


def kernel_back(images, pre_grad):
    batch, side = (images.shape[0], images.shape[1])
    padded = jnp.pad(images, ((0, 0), (1, 1), (1, 1), (0, 0))).reshape(
        batch, side + 2, side + 2, GROUPS, CG
    )
    upstream = pre_grad.reshape(batch, side, side, GROUPS, CG)
    terms = []
    for tap_index in range(9):
        row_off, col_off = (tap_index // 3, tap_index % 3)
        window = padded[:, row_off : row_off + side, col_off : col_off + side]
        terms.append(
            jnp.einsum("bhwgc,bhwgd->gdc", window, upstream, preferred_element_type=jnp.float32)
        )
    return jnp.stack(terms, axis=2).reshape(GROUPS * CG * 9 * CG)


def channel_scale(sum_plain, sum_square, channel_gain):
    chan_mean = sum_plain / FAN
    chan_var = sum_square / FAN - chan_mean * chan_mean
    return (chan_mean, channel_gain / jnp.sqrt(FAN * chan_var + 0.0001))


def adam(grad, master, mean, square):
    mean_next = 0.9 * mean + 0.1 * grad
    square_next = 0.999 * square + 0.001 * grad * grad
    fix_mean = 1.0 - 0.9**ADAM_STEP
    fix_square = 1.0 - 0.999**ADAM_STEP
    update = mean_next / fix_mean / (jnp.sqrt(square_next / fix_square) + 1e-08)
    return (master - 0.02 * update, mean_next, square_next)


def on_device(
    activations, cotangent, kernel, channel_gain, master_flat, moment_mean, moment_square
):
    kernel_taps = kernel.reshape(GROUPS, CG, 9, CG)
    preact = forward(activations, kernel_taps)
    pre_grad = (cotangent.astype(jnp.float32) * gelu_slope(preact)).astype(jnp.bfloat16)
    grad_full = kernel_back(activations, pre_grad)
    grad_shard = lax.psum_scatter(grad_full, ("dp", "sub"), scatter_dimension=0, tiled=True)
    input_grad = input_back(pre_grad, kernel_taps).astype(jnp.bfloat16)
    master_next, mean_next, square_next = adam(
        grad_shard, master_flat, moment_mean, moment_square
    )
    shard_len = master_next.shape[0]
    shard_start = lax.axis_index(("dp", "sub")) * shard_len
    first_chan = shard_start // FAN
    chan_span = shard_len // FAN + 2
    offsets = shard_start + jnp.arange(shard_len, dtype=jnp.int32)
    local_chan = offsets // FAN - first_chan
    onehot = (local_chan[:, None] == jnp.arange(chan_span, dtype=jnp.int32)[None, :]).astype(
        jnp.float32
    )
    highest = lax.Precision.HIGHEST
    plain_part = jnp.dot(master_next, onehot, precision=highest)
    square_part = jnp.dot(master_next * master_next, onehot, precision=highest)
    empty = jnp.zeros((CMID + chan_span,), jnp.float32)
    plain_full = lax.dynamic_update_slice(empty, plain_part, (first_chan,))[:CMID]
    square_full = lax.dynamic_update_slice(empty, square_part, (first_chan,))[:CMID]
    sum_plain, sum_square = lax.psum((plain_full, square_full), ("dp", "sub"))
    chan_mean, chan_scale = channel_scale(sum_plain, sum_square, channel_gain)
    mean_window = lax.dynamic_slice(
        jnp.concatenate([chan_mean, empty[:chan_span]]), (first_chan,), (chan_span,)
    )
    scale_window = lax.dynamic_slice(
        jnp.concatenate([chan_scale, empty[:chan_span]]), (first_chan,), (chan_span,)
    )
    entry_mean = jnp.dot(onehot, mean_window, precision=highest)
    entry_scale = jnp.dot(onehot, scale_window, precision=highest)
    standard_shard = ((master_next - entry_mean) * entry_scale).astype(jnp.bfloat16)
    kernel_next = lax.all_gather(standard_shard, ("dp", "sub"), axis=0, tiled=True).reshape(
        CMID, FAN
    )
    return (input_grad, master_next, mean_next, square_next, kernel_next)


MESH = pl.DeviceIdType.MESH
SHARD_ROWS = 12
LINES = SHARD_ROWS * 9
SLOT = 112
F32 = jnp.float32
BF16 = jnp.bfloat16


def step_kernel(
    act, cot, ker, gain, master, mean, square,
    back, grad_out, ker_out,
    pad32, cot32, xl, gl, gf, gb, r1, s1, r2, s2, r3, s3, r4, kb, kf, rows_in, rows_out,
    rs_send, rs_recv, ag_send, ag_recv,
):
    dp = lax.axis_index("dp")
    x = lax.axis_index("sub")
    z, y, c = lax.div(dp, 4), lax.rem(lax.div(dp, 2), 2), lax.rem(dp, 2)
    core_dev = (dp + 1 - 2 * c, x)
    x_dev = (dp, 1 - x)
    y_dev = (dp + 2 - 4 * y, x)

    def z_dev(other):
        return (other * 4 + lax.rem(dp, 4), x)

    def ahead(k):
        return lax.rem(z + k, 4)

    def behind(k):
        return lax.rem(z + 4 - k, 4)

    barrier = pltpu.get_barrier_semaphore()
    for device in (core_dev, x_dev, y_dev, z_dev(ahead(1)), z_dev(ahead(2)), z_dev(ahead(3))):
        pl.semaphore_signal(barrier, inc=1, device_id=device, device_id_type=MESH)

    pad32[:, :, 8:16, :] = jnp.zeros((2, 14, 8, CMID), F32)
    cot32[:, :, 8:16, :] = jnp.zeros((2, 14, 8, CMID), F32)
    pad32[:, :, 0:14, :] = act[...].astype(F32)
    cot32[:, :, 0:14, :] = cot[...].astype(F32)
    for edge in (0, 15):
        xl[:, edge] = jnp.zeros((2, 16, 9 * CG), BF16)
        gl[:, edge] = jnp.zeros((2, 16, 9 * CG), BF16)
    gf[3456:3472, :] = jnp.zeros((16, CG), F32)

    def shifted(values, by):
        return values if by == 0 else pltpu.roll(values, by % 448, 0)

    def grid(values):
        return values.astype(BF16).reshape(2, 14, 16, CG)

    def window(ref, top, g):
        return ref[:, top : top + 14, :, g * 384 : g * 384 + 384].reshape(448, 384)

    for g in range(GROUPS):
        chans = slice(g * CG, g * CG + CG)
        image = pad32[:, :, :, chans].reshape(448, CG)
        for kx in range(3):
            at = g * 384 + kx * CG
            xl[:, 1:15, :, at : at + CG] = grid(shifted(image, 1 - kx))
        preact = jnp.zeros((448, CG), F32)
        for ky in range(3):
            preact += lax.dot_general(
                window(xl, ky, g), ker[chans, ky * 384 : ky * 384 + 384],
                (((1,), (1,)), ((), ())), preferred_element_type=F32,
            )
        rounded = (cot32[:, :, :, chans].reshape(448, CG) * gelu_slope(preact)).astype(BF16)
        wide = rounded.astype(F32)
        for kx in range(3):
            at = g * 384 + kx * CG
            gl[:, 1:15, :, at : at + CG] = grid(shifted(wide, kx - 1))
        turned = wide.T.astype(BF16)
        for ky in range(3):
            part = jnp.dot(turned, window(xl, ky, g), preferred_element_type=F32)
            for kx in range(3):
                line = g * 9 * CG + ky * 3 + kx
                gf[pl.ds(line, CG, stride=9), :] = part[:, kx * CG : kx * CG + CG]

    for zc in range(4):
        for yc in range(2):
            for cc in range(2):
                for xc in range(2):
                    first = (((zc * 2 + yc) * 2 + cc) * 2 + xc) * LINES
                    gb[zc, cc, yc, xc] = gf[first : first + SLOT, :].astype(BF16)

    def input_back_group(g):
        chans = slice(g * CG, g * CG + CG)
        total = jnp.zeros((448, CG), F32)
        for ky in range(3):
            taps = [ker[chans, (ky * 3 + kx) * CG : (ky * 3 + kx) * CG + CG] for kx in range(3)]
            total += jnp.dot(
                window(gl, 2 - ky, g), jnp.concatenate(taps, axis=0), preferred_element_type=F32
            )
        back[:, :, :, chans] = total.reshape(2, 14, 16, CG)[:, :, 0:14, :].astype(BF16)

    def send(src, dst, send_sem, recv_sem, device):
        copy = pltpu.make_async_remote_copy(
            src_ref=src, dst_ref=dst, send_sem=send_sem, recv_sem=recv_sem,
            device_id=device, device_id_type=MESH,
        )
        copy.start()
        return copy

    def both(one, other):
        return one.astype(F32) + other.astype(F32)

    pl.semaphore_wait(barrier, 6)
    order = (2, 1, 3, 0)
    copies = {}
    for k in order:
        copies[1, k] = send(
            gb.at[ahead(k), 1 - c], r1.at[k], rs_send.at[0, k], rs_recv.at[0, k], core_dev
        )
    input_back_group(0)
    for k in order:
        copies[1, k].wait_recv()
        zc = ahead(k)
        for yc in range(2):
            for xc in range(2):
                one, two = (xc, yc) if k % 2 == 0 else (yc, xc)
                s1[k, one, two] = both(gb[zc, c, yc, xc], r1[k, yc, xc]).astype(BF16)
        mine, device = (x, x_dev) if k % 2 == 0 else (y, y_dev)
        copies[2, k] = send(
            s1.at[k, 1 - mine], r2.at[k], rs_send.at[1, k], rs_recv.at[1, k], device
        )
    input_back_group(1)
    for k in order:
        copies[2, k].wait_recv()
        one, two, device = (x, y, y_dev) if k % 2 == 0 else (y, x, x_dev)
        for b in range(2):
            s2[k, b] = both(s1[k, one, b], r2[k, b]).astype(BF16)
        copies[3, k] = send(
            s2.at[k, 1 - two], r3.at[k], rs_send.at[2, k], rs_recv.at[2, k], device
        )
    input_back_group(2)
    for k in order:
        copies[3, k].wait_recv()
        two = y if k % 2 == 0 else x
        if k != 0:
            s3[k] = both(s2[k, two], r3[k]).astype(BF16)
            copies[4, k] = send(
                s3.at[k], r4.at[k], rs_send.at[3, k], rs_recv.at[3, k], z_dev(ahead(k))
            )
    grad = both(s2[0, y], r3[0])
    for k in (1, 3, 2):
        copies[4, k].wait_recv()
        grad = grad + r4[k].astype(F32)
    grad = grad[0:LINES, :]
    grad_out[...] = grad

    master_next, _, _ = adam(grad, master[...], mean[...], square[...])
    rows_in[0:LINES, :] = master_next
    taps = [rows_in[pl.ds(t, SHARD_ROWS, stride=9), :] for t in range(9)]
    plain, squares = taps[0], taps[0] * taps[0]
    for tap in taps[1:]:
        plain, squares = plain + tap, squares + tap * tap
    shape = (SHARD_ROWS, CG)
    first_chan = (dp * 2 + x) * SHARD_ROWS
    chan = lax.broadcasted_iota(jnp.int32, shape, 0) + first_chan
    lane = lax.broadcasted_iota(jnp.int32, shape, 1)
    picked = jnp.zeros(shape, F32)
    for g in range(GROUPS):
        picked += jnp.where(lane + g * CG == chan, gain[g : g + 1, :], 0.0)
    own_gain = jnp.sum(picked, axis=1, keepdims=True)
    chan_mean, chan_scale = channel_scale(
        jnp.sum(plain, axis=1, keepdims=True), jnp.sum(squares, axis=1, keepdims=True), own_gain
    )
    rows_out[104:SLOT, :] = jnp.zeros((8, CG), F32)
    for t in range(9):
        rows_out[pl.ds(t, SHARD_ROWS, stride=9), :] = (taps[t] - chan_mean) * chan_scale
    kb[z, c, y, x] = rows_out[...].astype(BF16)

    own_slot = kb.at[z, c, y, x]
    for k in (2, 1, 3):
        copies[5, k] = send(
            own_slot, own_slot, ag_send.at[0, k], ag_recv.at[0, k], z_dev(ahead(k))
        )
    order = (0, 1, 3, 2)
    for k in order:
        if k != 0:
            copies[5, k].wait_recv()
        slot = kb.at[behind(k), c, y, x]
        copies[6, k] = send(
            slot, slot, ag_send.at[1, k], ag_recv.at[1, k], x_dev if k % 2 == 0 else y_dev
        )
    for k in order:
        copies[6, k].wait_recv()
        zc = behind(k)
        slot = kb.at[zc, c, y] if k % 2 == 0 else kb.at[zc, c, :, x]
        copies[7, k] = send(
            slot, slot, ag_send.at[2, k], ag_recv.at[2, k], y_dev if k % 2 == 0 else x_dev
        )
    for k in order:
        copies[7, k].wait_recv()
        slot = kb.at[behind(k), c]
        copies[8, k] = send(slot, slot, ag_send.at[3, k], ag_recv.at[3, k], core_dev)
    for k in order:
        copies[8, k].wait_recv()
        zc = behind(k)
        for yc in range(2):
            for cc in range(2):
                for xc in range(2):
                    first = ((yc * 2 + cc) * 2 + xc) * LINES
                    kf[first : first + LINES, :] = kb[zc, cc, yc, xc].astype(F32)[0:LINES, :]
        rows = pl.ds(pl.multiple_of(zc * 96, 96), 96)
        for t in range(9):
            ker_out[rows, t * CG : t * CG + CG] = kf[pl.ds(t, 96, stride=9), :].astype(BF16)
    for copy in copies.values():
        copy.wait_send()


def fused_on_device(
    activations, cotangent, kernel, channel_gain, master_flat, moment_mean, moment_square
):
    vmem = pl.BlockSpec(memory_space=pltpu.VMEM)
    back, grad, kernel_next = pl.pallas_call(
        step_kernel,
        out_shape=(
            jax.ShapeDtypeStruct(activations.shape, BF16),
            jax.ShapeDtypeStruct((LINES, CG), F32),
            jax.ShapeDtypeStruct((CMID, FAN), BF16),
        ),
        in_specs=[vmem] * 7,
        out_specs=(vmem,) * 3,
        scratch_shapes=[
            pltpu.VMEM((2, 14, 16, CMID), F32),
            pltpu.VMEM((2, 14, 16, CMID), F32),
            pltpu.VMEM((2, 16, 16, 9 * CG), BF16),
            pltpu.VMEM((2, 16, 16, 9 * CG), BF16),
            pltpu.VMEM((3472, CG), F32),
            pltpu.VMEM((4, 2, 2, 2, SLOT, CG), BF16),
            pltpu.VMEM((4, 2, 2, SLOT, CG), BF16),
            pltpu.VMEM((4, 2, 2, SLOT, CG), BF16),
            pltpu.VMEM((4, 2, SLOT, CG), BF16),
            pltpu.VMEM((4, 2, SLOT, CG), BF16),
            pltpu.VMEM((4, SLOT, CG), BF16),
            pltpu.VMEM((4, SLOT, CG), BF16),
            pltpu.VMEM((4, SLOT, CG), BF16),
            pltpu.VMEM((4, 2, 2, 2, SLOT, CG), BF16),
            pltpu.VMEM((96 * 9, CG), F32),
            pltpu.VMEM((SLOT, CG), F32),
            pltpu.VMEM((SLOT, CG), F32),
            pltpu.SemaphoreType.DMA((4, 4)),
            pltpu.SemaphoreType.DMA((4, 4)),
            pltpu.SemaphoreType.DMA((4, 4)),
            pltpu.SemaphoreType.DMA((4, 4)),
        ],
        compiler_params=pltpu.CompilerParams(
            collective_id=0, has_side_effects=True, vmem_limit_bytes=40 * 1024 * 1024
        ),
        cost_estimate=pl.CostEstimate(
            flops=1_100_000_000, bytes_accessed=4_000_000, transcendentals=400_000
        ),
    )(
        activations, cotangent, kernel, channel_gain.reshape(GROUPS, CG),
        master_flat.reshape(LINES, CG), moment_mean.reshape(LINES, CG),
        moment_square.reshape(LINES, CG),
    )
    master_next, mean_next, square_next = adam(
        grad.reshape(-1), master_flat, moment_mean, moment_square
    )
    return (back, master_next, mean_next, square_next, kernel_next)


def solution(mesh):
    placed = (
        P(("dp", "sub"), None, None, None),
        P(("dp", "sub"), None, None, None),
        P(),
        P(),
        P(("dp", "sub")),
        P(("dp", "sub")),
        P(("dp", "sub")),
    )
    fused = dict(mesh.shape) == {"dp": 16, "sub": 2}
    return jax.shard_map(
        fused_on_device if fused else on_device,
        mesh=mesh,
        in_specs=placed,
        out_specs=(
            P(("dp", "sub"), None, None, None),
            P(("dp", "sub")),
            P(("dp", "sub")),
            P(("dp", "sub")),
            P(),
        ),
        check_vma=False,
    )
```

```python
import jax
import jax.numpy as jnp
from jax import lax
from jax.experimental import pallas as pl
from jax.experimental.pallas import tpu as pltpu
from jax.sharding import PartitionSpec as P

CMID = 384
CG = 128
ADAM_STEP = 10
GROUPS = 3
FAN = 1152


HALF_ROOT = 0.7071067811865476
INV_ROOT_TAU = 0.3989422804014327


def gelu_slope(values):
    return (
        0.5 * (1.0 + lax.erf(values * HALF_ROOT))
        + values * jnp.exp(-0.5 * values * values) * INV_ROOT_TAU
    )


def forward(images, kernel_taps):
    batch, side = (images.shape[0], images.shape[1])
    padded = jnp.pad(images, ((0, 0), (1, 1), (1, 1), (0, 0))).reshape(
        batch, side + 2, side + 2, GROUPS, CG
    )
    total = jnp.zeros((batch, side, side, GROUPS, CG), jnp.float32)
    for tap_index in range(9):
        row_off, col_off = (tap_index // 3, tap_index % 3)
        window = padded[:, row_off : row_off + side, col_off : col_off + side]
        total = total + jnp.einsum(
            "bhwgc,gdc->bhwgd",
            window,
            kernel_taps[:, :, tap_index, :],
            preferred_element_type=jnp.float32,
        )
    return total.reshape(batch, side, side, GROUPS * CG)


def input_back(pre_grad, kernel_taps):
    batch, side = (pre_grad.shape[0], pre_grad.shape[1])
    padded = jnp.pad(pre_grad, ((0, 0), (1, 1), (1, 1), (0, 0))).reshape(
        batch, side + 2, side + 2, GROUPS, CG
    )
    total = jnp.zeros((batch, side, side, GROUPS, CG), jnp.float32)
    for tap_index in range(9):
        row_off, col_off = (tap_index // 3, tap_index % 3)
        window = padded[:, 2 - row_off : 2 - row_off + side, 2 - col_off : 2 - col_off + side]
        total = total + jnp.einsum(
            "bhwgd,gdc->bhwgc",
            window,
            kernel_taps[:, :, tap_index, :],
            preferred_element_type=jnp.float32,
        )
    return total.reshape(batch, side, side, GROUPS * CG)


def kernel_back(images, pre_grad):
    batch, side = (images.shape[0], images.shape[1])
    padded = jnp.pad(images, ((0, 0), (1, 1), (1, 1), (0, 0))).reshape(
        batch, side + 2, side + 2, GROUPS, CG
    )
    upstream = pre_grad.reshape(batch, side, side, GROUPS, CG)
    terms = []
    for tap_index in range(9):
        row_off, col_off = (tap_index // 3, tap_index % 3)
        window = padded[:, row_off : row_off + side, col_off : col_off + side]
        terms.append(
            jnp.einsum("bhwgc,bhwgd->gdc", window, upstream, preferred_element_type=jnp.float32)
        )
    return jnp.stack(terms, axis=2).reshape(GROUPS * CG * 9 * CG)


def channel_scale(sum_plain, sum_square, channel_gain):
    chan_mean = sum_plain / FAN
    chan_var = sum_square / FAN - chan_mean * chan_mean
    return (chan_mean, channel_gain / jnp.sqrt(FAN * chan_var + 0.0001))


def adam(grad, master, mean, square):
    mean_next = 0.9 * mean + 0.1 * grad
    square_next = 0.999 * square + 0.001 * grad * grad
    fix_mean = 1.0 - 0.9**ADAM_STEP
    fix_square = 1.0 - 0.999**ADAM_STEP
    update = mean_next / fix_mean / (jnp.sqrt(square_next / fix_square) + 1e-08)
    return (master - 0.02 * update, mean_next, square_next)


def on_device(
    activations, cotangent, kernel, channel_gain, master_flat, moment_mean, moment_square
):
    kernel_taps = kernel.reshape(GROUPS, CG, 9, CG)
    preact = forward(activations, kernel_taps)
    pre_grad = (cotangent.astype(jnp.float32) * gelu_slope(preact)).astype(jnp.bfloat16)
    grad_full = kernel_back(activations, pre_grad)
    grad_shard = lax.psum_scatter(grad_full, ("dp", "sub"), scatter_dimension=0, tiled=True)
    input_grad = input_back(pre_grad, kernel_taps).astype(jnp.bfloat16)
    master_next, mean_next, square_next = adam(
        grad_shard, master_flat, moment_mean, moment_square
    )
    shard_len = master_next.shape[0]
    shard_start = lax.axis_index(("dp", "sub")) * shard_len
    first_chan = shard_start // FAN
    chan_span = shard_len // FAN + 2
    offsets = shard_start + jnp.arange(shard_len, dtype=jnp.int32)
    local_chan = offsets // FAN - first_chan
    onehot = (local_chan[:, None] == jnp.arange(chan_span, dtype=jnp.int32)[None, :]).astype(
        jnp.float32
    )
    highest = lax.Precision.HIGHEST
    plain_part = jnp.dot(master_next, onehot, precision=highest)
    square_part = jnp.dot(master_next * master_next, onehot, precision=highest)
    empty = jnp.zeros((CMID + chan_span,), jnp.float32)
    plain_full = lax.dynamic_update_slice(empty, plain_part, (first_chan,))[:CMID]
    square_full = lax.dynamic_update_slice(empty, square_part, (first_chan,))[:CMID]
    sum_plain, sum_square = lax.psum((plain_full, square_full), ("dp", "sub"))
    chan_mean, chan_scale = channel_scale(sum_plain, sum_square, channel_gain)
    mean_window = lax.dynamic_slice(
        jnp.concatenate([chan_mean, empty[:chan_span]]), (first_chan,), (chan_span,)
    )
    scale_window = lax.dynamic_slice(
        jnp.concatenate([chan_scale, empty[:chan_span]]), (first_chan,), (chan_span,)
    )
    entry_mean = jnp.dot(onehot, mean_window, precision=highest)
    entry_scale = jnp.dot(onehot, scale_window, precision=highest)
    standard_shard = ((master_next - entry_mean) * entry_scale).astype(jnp.bfloat16)
    kernel_next = lax.all_gather(standard_shard, ("dp", "sub"), axis=0, tiled=True).reshape(
        CMID, FAN
    )
    return (input_grad, master_next, mean_next, square_next, kernel_next)


MESH = pl.DeviceIdType.MESH
SHARD_ROWS = 12
LINES = SHARD_ROWS * 9
SLOT = 112
F32 = jnp.float32
BF16 = jnp.bfloat16


def step_kernel(
    act, cot, ker, gain, master, mean, square,
    back, grad_out, ker_out,
    pad32, cot32, xl, gl, gf, gb, r1, s1, r2, s2, r3, s3, held, r4, kb, kf, rows_in, rows_out,
    rs_send, rs_recv, ag_send, ag_recv,
):
    dp = lax.axis_index("dp")
    x = lax.axis_index("sub")
    z, y, c = lax.div(dp, 4), lax.rem(lax.div(dp, 2), 2), lax.rem(dp, 2)
    core_dev = (dp + 1 - 2 * c, x)
    x_dev = (dp, 1 - x)
    y_dev = (dp + 2 - 4 * y, x)

    def z_dev(other):
        return (other * 4 + lax.rem(dp, 4), x)

    def ahead(k):
        return lax.rem(z + k, 4)

    def behind(k):
        return lax.rem(z + 4 - k, 4)

    barrier = pltpu.get_barrier_semaphore()
    for device in (core_dev, x_dev, y_dev, z_dev(ahead(1)), z_dev(ahead(2)), z_dev(ahead(3))):
        pl.semaphore_signal(barrier, inc=1, device_id=device, device_id_type=MESH)

    pad32[:, :, 8:16, :] = jnp.zeros((2, 14, 8, CMID), F32)
    cot32[:, :, 8:16, :] = jnp.zeros((2, 14, 8, CMID), F32)
    pad32[:, :, 0:14, :] = act[...].astype(F32)
    cot32[:, :, 0:14, :] = cot[...].astype(F32)
    for edge in (0, 15):
        xl[:, edge] = jnp.zeros((2, 16, 9 * CG), BF16)
        gl[:, edge] = jnp.zeros((2, 16, 9 * CG), BF16)
    gf[3456:3472, :] = jnp.zeros((16, CG), F32)

    def shifted(values, by):
        return values if by == 0 else pltpu.roll(values, by % 448, 0)

    def grid(values):
        return values.astype(BF16).reshape(2, 14, 16, CG)

    def window(ref, top, g):
        return ref[:, top : top + 14, :, g * 384 : g * 384 + 384].reshape(448, 384)

    def gradient_group(g):
        chans = slice(g * CG, g * CG + CG)
        image = pad32[:, :, :, chans].reshape(448, CG)
        for kx in range(3):
            at = g * 384 + kx * CG
            xl[:, 1:15, :, at : at + CG] = grid(shifted(image, 1 - kx))
        preact = jnp.zeros((448, CG), F32)
        for ky in range(3):
            preact += lax.dot_general(
                window(xl, ky, g), ker[chans, ky * 384 : ky * 384 + 384],
                (((1,), (1,)), ((), ())), preferred_element_type=F32,
            )
        rounded = (cot32[:, :, :, chans].reshape(448, CG) * gelu_slope(preact)).astype(BF16)
        wide = rounded.astype(F32)
        turned = wide.T.astype(BF16)
        for ky in range(3):
            part = jnp.dot(turned, window(xl, ky, g), preferred_element_type=F32)
            for kx in range(3):
                line = g * 9 * CG + ky * 3 + kx
                gf[pl.ds(line, CG, stride=9), :] = part[:, kx * CG : kx * CG + CG]
        for kx in range(3):
            at = g * 384 + kx * CG
            gl[:, 1:15, :, at : at + CG] = grid(shifted(wide, kx - 1))

    def input_back_group(g):
        chans = slice(g * CG, g * CG + CG)
        total = jnp.zeros((448, CG), F32)
        for ky in range(3):
            taps = [ker[chans, (ky * 3 + kx) * CG : (ky * 3 + kx) * CG + CG] for kx in range(3)]
            total += jnp.dot(
                window(gl, 2 - ky, g), jnp.concatenate(taps, axis=0), preferred_element_type=F32
            )
        back[:, :, :, chans] = total.reshape(2, 14, 16, CG)[:, :, 0:14, :].astype(BF16)

    def remote(src, dst, send_sem, recv_sem, device):
        return pltpu.make_async_remote_copy(
            src_ref=src, dst_ref=dst, send_sem=send_sem, recv_sem=recv_sem,
            device_id=device, device_id_type=MESH,
        )

    def send(*parts):
        copy = remote(*parts)
        copy.start()
        return copy

    def both(one, other):
        return one.astype(F32) + other.astype(F32)

    copies = {}

    def pair_stage(zc):
        for yc in range(2):
            for cc in range(2):
                for xc in range(2):
                    first = (((zc * 2 + yc) * 2 + cc) * 2 + xc) * LINES
                    gb[zc, cc, yc, xc] = gf[first : first + SLOT, :].astype(BF16)
        copies[1, zc] = send(
            gb.at[zc, 1 - c], r1.at[zc], rs_send.at[0, zc], rs_recv.at[0, zc], core_dev
        )

    def first_stage(zc):
        copies[1, zc].wait_recv()
        for yc in range(2):
            for xc in range(2):
                one, two = (xc, yc) if zc % 2 == 0 else (yc, xc)
                s1[zc, one, two] = both(gb[zc, c, yc, xc], r1[zc, yc, xc]).astype(BF16)
        mine, device = (x, x_dev) if zc % 2 == 0 else (y, y_dev)
        copies[2, zc] = send(
            s1.at[zc, 1 - mine], r2.at[zc], rs_send.at[1, zc], rs_recv.at[1, zc], device
        )

    def second_stage(zc):
        copies[2, zc].wait_recv()
        one, two, device = (x, y, y_dev) if zc % 2 == 0 else (y, x, x_dev)
        for b in range(2):
            s2[zc, b] = both(s1[zc, one, b], r2[zc, b]).astype(BF16)
        copies[3, zc] = send(
            s2.at[zc, 1 - two], r3.at[zc], rs_send.at[2, zc], rs_recv.at[2, zc], device
        )

    def line_copy(src_z, dst_z):
        return remote(
            s3.at[dst_z], r4.at[src_z], rs_send.at[3, dst_z], rs_recv.at[3, src_z], z_dev(dst_z)
        )

    def line_stage(zc):
        copies[3, zc].wait_recv()
        two = y if zc % 2 == 0 else x
        total = both(s2[zc, two], r3[zc])
        held[zc] = total
        s3[zc] = total.astype(BF16)

        @pl.when(z != zc)
        def _():
            line_copy(z, zc).start()

    gradient_group(0)
    gradient_group(1)
    pl.semaphore_wait(barrier, 6)
    pair_stage(0)
    pair_stage(1)
    gradient_group(2)
    pair_stage(2)
    pair_stage(3)
    first_stage(0)
    first_stage(1)
    input_back_group(0)
    first_stage(2)
    first_stage(3)
    second_stage(0)
    second_stage(1)
    input_back_group(1)
    line_stage(0)
    line_stage(1)
    second_stage(2)
    second_stage(3)
    input_back_group(2)
    line_stage(2)
    line_stage(3)
    grad = held[z]
    for k in (1, 3, 2):
        line_copy(ahead(k), ahead(k)).wait_recv()
        grad = grad + r4[ahead(k)].astype(F32)
    grad = grad[0:LINES, :]
    grad_out[...] = grad

    master_next, _, _ = adam(grad, master[...], mean[...], square[...])
    rows_in[0:LINES, :] = master_next
    taps = [rows_in[pl.ds(t, SHARD_ROWS, stride=9), :] for t in range(9)]
    plain, squares = taps[0], taps[0] * taps[0]
    for tap in taps[1:]:
        plain, squares = plain + tap, squares + tap * tap
    shape = (SHARD_ROWS, CG)
    first_chan = (dp * 2 + x) * SHARD_ROWS
    chan = lax.broadcasted_iota(jnp.int32, shape, 0) + first_chan
    lane = lax.broadcasted_iota(jnp.int32, shape, 1)
    picked = jnp.zeros(shape, F32)
    for g in range(GROUPS):
        picked += jnp.where(lane + g * CG == chan, gain[g : g + 1, :], 0.0)
    own_gain = jnp.sum(picked, axis=1, keepdims=True)
    chan_mean, chan_scale = channel_scale(
        jnp.sum(plain, axis=1, keepdims=True), jnp.sum(squares, axis=1, keepdims=True), own_gain
    )
    rows_out[104:SLOT, :] = jnp.zeros((8, CG), F32)
    for t in range(9):
        rows_out[pl.ds(t, SHARD_ROWS, stride=9), :] = (taps[t] - chan_mean) * chan_scale
    kb[z, c, y, x] = rows_out[...].astype(BF16)

    own_slot = kb.at[z, c, y, x]
    for k in (2, 1, 3):
        copies[5, k] = send(
            own_slot, own_slot, ag_send.at[0, k], ag_recv.at[0, k], z_dev(ahead(k))
        )
    order = (0, 1, 3, 2)
    for k in order:
        if k != 0:
            copies[5, k].wait_recv()
        slot = kb.at[behind(k), c, y, x]
        copies[6, k] = send(
            slot, slot, ag_send.at[1, k], ag_recv.at[1, k], x_dev if k % 2 == 0 else y_dev
        )
    for k in order:
        copies[6, k].wait_recv()
        zc = behind(k)
        slot = kb.at[zc, c, y] if k % 2 == 0 else kb.at[zc, c, :, x]
        copies[7, k] = send(
            slot, slot, ag_send.at[2, k], ag_recv.at[2, k], y_dev if k % 2 == 0 else x_dev
        )
    for k in order:
        copies[7, k].wait_recv()
        slot = kb.at[behind(k), c]
        copies[8, k] = send(slot, slot, ag_send.at[3, k], ag_recv.at[3, k], core_dev)
    for k in order:
        copies[8, k].wait_recv()
        zc = behind(k)
        for yc in range(2):
            for cc in range(2):
                for xc in range(2):
                    first = ((yc * 2 + cc) * 2 + xc) * LINES
                    kf[first : first + LINES, :] = kb[zc, cc, yc, xc].astype(F32)[0:LINES, :]
        rows = pl.ds(pl.multiple_of(zc * 96, 96), 96)
        for t in range(9):
            ker_out[rows, t * CG : t * CG + CG] = kf[pl.ds(t, 96, stride=9), :].astype(BF16)
    for copy in copies.values():
        copy.wait_send()
    for k in range(1, 4):
        line_copy(z, ahead(k)).wait_send()


def fused_on_device(
    activations, cotangent, kernel, channel_gain, master_flat, moment_mean, moment_square
):
    vmem = pl.BlockSpec(memory_space=pltpu.VMEM)
    back, grad, kernel_next = pl.pallas_call(
        step_kernel,
        out_shape=(
            jax.ShapeDtypeStruct(activations.shape, BF16),
            jax.ShapeDtypeStruct((LINES, CG), F32),
            jax.ShapeDtypeStruct((CMID, FAN), BF16),
        ),
        in_specs=[vmem] * 7,
        out_specs=(vmem,) * 3,
        scratch_shapes=[
            pltpu.VMEM((2, 14, 16, CMID), F32),
            pltpu.VMEM((2, 14, 16, CMID), F32),
            pltpu.VMEM((2, 16, 16, 9 * CG), BF16),
            pltpu.VMEM((2, 16, 16, 9 * CG), BF16),
            pltpu.VMEM((3472, CG), F32),
            pltpu.VMEM((4, 2, 2, 2, SLOT, CG), BF16),
            pltpu.VMEM((4, 2, 2, SLOT, CG), BF16),
            pltpu.VMEM((4, 2, 2, SLOT, CG), BF16),
            pltpu.VMEM((4, 2, SLOT, CG), BF16),
            pltpu.VMEM((4, 2, SLOT, CG), BF16),
            pltpu.VMEM((4, SLOT, CG), BF16),
            pltpu.VMEM((4, SLOT, CG), BF16),
            pltpu.VMEM((4, SLOT, CG), F32),
            pltpu.VMEM((4, SLOT, CG), BF16),
            pltpu.VMEM((4, 2, 2, 2, SLOT, CG), BF16),
            pltpu.VMEM((96 * 9, CG), F32),
            pltpu.VMEM((SLOT, CG), F32),
            pltpu.VMEM((SLOT, CG), F32),
            pltpu.SemaphoreType.DMA((4, 4)),
            pltpu.SemaphoreType.DMA((4, 4)),
            pltpu.SemaphoreType.DMA((4, 4)),
            pltpu.SemaphoreType.DMA((4, 4)),
        ],
        compiler_params=pltpu.CompilerParams(
            collective_id=0, has_side_effects=True, vmem_limit_bytes=40 * 1024 * 1024
        ),
        cost_estimate=pl.CostEstimate(
            flops=1_100_000_000, bytes_accessed=4_000_000, transcendentals=400_000
        ),
    )(
        activations, cotangent, kernel, channel_gain.reshape(GROUPS, CG),
        master_flat.reshape(LINES, CG), moment_mean.reshape(LINES, CG),
        moment_square.reshape(LINES, CG),
    )
    master_next, mean_next, square_next = adam(
        grad.reshape(-1), master_flat, moment_mean, moment_square
    )
    return (back, master_next, mean_next, square_next, kernel_next)


def solution(mesh):
    placed = (
        P(("dp", "sub"), None, None, None),
        P(("dp", "sub"), None, None, None),
        P(),
        P(),
        P(("dp", "sub")),
        P(("dp", "sub")),
        P(("dp", "sub")),
    )
    fused = dict(mesh.shape) == {"dp": 16, "sub": 2}
    return jax.shard_map(
        fused_on_device if fused else on_device,
        mesh=mesh,
        in_specs=placed,
        out_specs=(
            P(("dp", "sub"), None, None, None),
            P(("dp", "sub")),
            P(("dp", "sub")),
            P(("dp", "sub")),
            P(),
        ),
        check_vma=False,
    )
```

```python
import jax
import jax.numpy as jnp
from jax import lax
from jax.experimental import pallas as pl
from jax.experimental.pallas import tpu as pltpu
from jax.sharding import PartitionSpec as P

CMID = 384
CG = 128
ADAM_STEP = 10
GROUPS = 3
FAN = 1152


HALF_ROOT = 0.7071067811865476
INV_ROOT_TAU = 0.3989422804014327


def gelu_slope(values):
    return (
        0.5 * (1.0 + lax.erf(values * HALF_ROOT))
        + values * jnp.exp(-0.5 * values * values) * INV_ROOT_TAU
    )


def forward(images, kernel_taps):
    batch, side = (images.shape[0], images.shape[1])
    padded = jnp.pad(images, ((0, 0), (1, 1), (1, 1), (0, 0))).reshape(
        batch, side + 2, side + 2, GROUPS, CG
    )
    total = jnp.zeros((batch, side, side, GROUPS, CG), jnp.float32)
    for tap_index in range(9):
        row_off, col_off = (tap_index // 3, tap_index % 3)
        window = padded[:, row_off : row_off + side, col_off : col_off + side]
        total = total + jnp.einsum(
            "bhwgc,gdc->bhwgd",
            window,
            kernel_taps[:, :, tap_index, :],
            preferred_element_type=jnp.float32,
        )
    return total.reshape(batch, side, side, GROUPS * CG)


def input_back(pre_grad, kernel_taps):
    batch, side = (pre_grad.shape[0], pre_grad.shape[1])
    padded = jnp.pad(pre_grad, ((0, 0), (1, 1), (1, 1), (0, 0))).reshape(
        batch, side + 2, side + 2, GROUPS, CG
    )
    total = jnp.zeros((batch, side, side, GROUPS, CG), jnp.float32)
    for tap_index in range(9):
        row_off, col_off = (tap_index // 3, tap_index % 3)
        window = padded[:, 2 - row_off : 2 - row_off + side, 2 - col_off : 2 - col_off + side]
        total = total + jnp.einsum(
            "bhwgd,gdc->bhwgc",
            window,
            kernel_taps[:, :, tap_index, :],
            preferred_element_type=jnp.float32,
        )
    return total.reshape(batch, side, side, GROUPS * CG)


def kernel_back(images, pre_grad):
    batch, side = (images.shape[0], images.shape[1])
    padded = jnp.pad(images, ((0, 0), (1, 1), (1, 1), (0, 0))).reshape(
        batch, side + 2, side + 2, GROUPS, CG
    )
    upstream = pre_grad.reshape(batch, side, side, GROUPS, CG)
    terms = []
    for tap_index in range(9):
        row_off, col_off = (tap_index // 3, tap_index % 3)
        window = padded[:, row_off : row_off + side, col_off : col_off + side]
        terms.append(
            jnp.einsum("bhwgc,bhwgd->gdc", window, upstream, preferred_element_type=jnp.float32)
        )
    return jnp.stack(terms, axis=2).reshape(GROUPS * CG * 9 * CG)


def channel_scale(sum_plain, sum_square, channel_gain):
    chan_mean = sum_plain / FAN
    chan_var = sum_square / FAN - chan_mean * chan_mean
    return (chan_mean, channel_gain / jnp.sqrt(FAN * chan_var + 0.0001))


def adam(grad, master, mean, square):
    mean_next = 0.9 * mean + 0.1 * grad
    square_next = 0.999 * square + 0.001 * grad * grad
    fix_mean = 1.0 - 0.9**ADAM_STEP
    fix_square = 1.0 - 0.999**ADAM_STEP
    update = mean_next / fix_mean / (jnp.sqrt(square_next / fix_square) + 1e-08)
    return (master - 0.02 * update, mean_next, square_next)


def on_device(
    activations, cotangent, kernel, channel_gain, master_flat, moment_mean, moment_square
):
    kernel_taps = kernel.reshape(GROUPS, CG, 9, CG)
    preact = forward(activations, kernel_taps)
    pre_grad = (cotangent.astype(jnp.float32) * gelu_slope(preact)).astype(jnp.bfloat16)
    grad_full = kernel_back(activations, pre_grad)
    grad_shard = lax.psum_scatter(grad_full, ("dp", "sub"), scatter_dimension=0, tiled=True)
    input_grad = input_back(pre_grad, kernel_taps).astype(jnp.bfloat16)
    master_next, mean_next, square_next = adam(
        grad_shard, master_flat, moment_mean, moment_square
    )
    shard_len = master_next.shape[0]
    shard_start = lax.axis_index(("dp", "sub")) * shard_len
    first_chan = shard_start // FAN
    chan_span = shard_len // FAN + 2
    offsets = shard_start + jnp.arange(shard_len, dtype=jnp.int32)
    local_chan = offsets // FAN - first_chan
    onehot = (local_chan[:, None] == jnp.arange(chan_span, dtype=jnp.int32)[None, :]).astype(
        jnp.float32
    )
    highest = lax.Precision.HIGHEST
    plain_part = jnp.dot(master_next, onehot, precision=highest)
    square_part = jnp.dot(master_next * master_next, onehot, precision=highest)
    empty = jnp.zeros((CMID + chan_span,), jnp.float32)
    plain_full = lax.dynamic_update_slice(empty, plain_part, (first_chan,))[:CMID]
    square_full = lax.dynamic_update_slice(empty, square_part, (first_chan,))[:CMID]
    sum_plain, sum_square = lax.psum((plain_full, square_full), ("dp", "sub"))
    chan_mean, chan_scale = channel_scale(sum_plain, sum_square, channel_gain)
    mean_window = lax.dynamic_slice(
        jnp.concatenate([chan_mean, empty[:chan_span]]), (first_chan,), (chan_span,)
    )
    scale_window = lax.dynamic_slice(
        jnp.concatenate([chan_scale, empty[:chan_span]]), (first_chan,), (chan_span,)
    )
    entry_mean = jnp.dot(onehot, mean_window, precision=highest)
    entry_scale = jnp.dot(onehot, scale_window, precision=highest)
    standard_shard = ((master_next - entry_mean) * entry_scale).astype(jnp.bfloat16)
    kernel_next = lax.all_gather(standard_shard, ("dp", "sub"), axis=0, tiled=True).reshape(
        CMID, FAN
    )
    return (input_grad, master_next, mean_next, square_next, kernel_next)


MESH = pl.DeviceIdType.MESH
SHARD_ROWS = 12
LINES = SHARD_ROWS * 9
SLOT = 112
F32 = jnp.float32
BF16 = jnp.bfloat16


def step_kernel(
    act, cot, ker, gain, master, mean, square,
    back, grad_out, ker_out,
    pad32, cot32, xl, gl, gf, gb, r1, s1, r2, s2, r3, s3, r4, kb, kf, rows_in, rows_out,
    rs_send, rs_recv, ag_send, ag_recv,
):
    dp = lax.axis_index("dp")
    x = lax.axis_index("sub")
    z, y, c = lax.div(dp, 4), lax.rem(lax.div(dp, 2), 2), lax.rem(dp, 2)
    core_dev = (dp + 1 - 2 * c, x)
    x_dev = (dp, 1 - x)
    y_dev = (dp + 2 - 4 * y, x)

    def z_dev(other):
        return (other * 4 + lax.rem(dp, 4), x)

    def ahead(k):
        return lax.rem(z + k, 4)

    def behind(k):
        return lax.rem(z + 4 - k, 4)

    barrier = pltpu.get_barrier_semaphore()
    for device in (core_dev, x_dev, y_dev, z_dev(ahead(1)), z_dev(ahead(2)), z_dev(ahead(3))):
        pl.semaphore_signal(barrier, inc=1, device_id=device, device_id_type=MESH)

    pad32[:, :, 8:16, :] = jnp.zeros((2, 14, 8, CMID), F32)
    cot32[:, :, 8:16, :] = jnp.zeros((2, 14, 8, CMID), F32)
    pad32[:, :, 0:14, :] = act[...].astype(F32)
    cot32[:, :, 0:14, :] = cot[...].astype(F32)
    for edge in (0, 15):
        xl[:, edge] = jnp.zeros((2, 16, 9 * CG), BF16)
        gl[:, edge] = jnp.zeros((2, 16, 9 * CG), BF16)
    gf[3456:3472, :] = jnp.zeros((16, CG), F32)

    def shifted(values, by):
        return values if by == 0 else pltpu.roll(values, by % 448, 0)

    def grid(values):
        return values.astype(BF16).reshape(2, 14, 16, CG)

    def window(ref, top, g):
        return ref[:, top : top + 14, :, g * 384 : g * 384 + 384].reshape(448, 384)

    for g in range(GROUPS):
        chans = slice(g * CG, g * CG + CG)
        image = pad32[:, :, :, chans].reshape(448, CG)
        for kx in range(3):
            at = g * 384 + kx * CG
            xl[:, 1:15, :, at : at + CG] = grid(shifted(image, 1 - kx))
        windows = jnp.concatenate([window(xl, ky, g) for ky in range(3)], axis=1)
        preact = lax.dot_general(
            windows, ker[chans, :], (((1,), (1,)), ((), ())), preferred_element_type=F32
        )
        rounded = (cot32[:, :, :, chans].reshape(448, CG) * gelu_slope(preact)).astype(BF16)
        wide = rounded.astype(F32)
        for kx in range(3):
            at = g * 384 + kx * CG
            gl[:, 1:15, :, at : at + CG] = grid(shifted(wide, kx - 1))
        turned = wide.T.astype(BF16)
        part = jnp.dot(turned, windows, preferred_element_type=F32)
        for tap in range(9):
            gf[pl.ds(g * 9 * CG + tap, CG, stride=9), :] = part[:, tap * CG : tap * CG + CG]

    for zc in range(4):
        for yc in range(2):
            for cc in range(2):
                for xc in range(2):
                    first = (((zc * 2 + yc) * 2 + cc) * 2 + xc) * LINES
                    gb[zc, cc, yc, xc] = gf[first : first + SLOT, :].astype(BF16)

    def input_back_group(g):
        chans = slice(g * CG, g * CG + CG)
        windows = jnp.concatenate([window(gl, 2 - ky, g) for ky in range(3)], axis=1)
        taps = [ker[chans, tap * CG : tap * CG + CG] for tap in range(9)]
        total = jnp.dot(windows, jnp.concatenate(taps, axis=0), preferred_element_type=F32)
        back[:, :, :, chans] = total.reshape(2, 14, 16, CG)[:, :, 0:14, :].astype(BF16)

    def send(src, dst, send_sem, recv_sem, device):
        copy = pltpu.make_async_remote_copy(
            src_ref=src, dst_ref=dst, send_sem=send_sem, recv_sem=recv_sem,
            device_id=device, device_id_type=MESH,
        )
        copy.start()
        return copy

    def both(one, other):
        return one.astype(F32) + other.astype(F32)

    pl.semaphore_wait(barrier, 6)
    order = (2, 1, 3, 0)
    copies = {}
    for k in order:
        copies[1, k] = send(
            gb.at[ahead(k), 1 - c], r1.at[k], rs_send.at[0, k], rs_recv.at[0, k], core_dev
        )
    input_back_group(0)
    for k in order:
        copies[1, k].wait_recv()
        zc = ahead(k)
        for yc in range(2):
            for xc in range(2):
                one, two = (xc, yc) if k % 2 == 0 else (yc, xc)
                s1[k, one, two] = both(gb[zc, c, yc, xc], r1[k, yc, xc]).astype(BF16)
        mine, device = (x, x_dev) if k % 2 == 0 else (y, y_dev)
        copies[2, k] = send(
            s1.at[k, 1 - mine], r2.at[k], rs_send.at[1, k], rs_recv.at[1, k], device
        )
    input_back_group(1)
    for k in order:
        copies[2, k].wait_recv()
        one, two, device = (x, y, y_dev) if k % 2 == 0 else (y, x, x_dev)
        for b in range(2):
            s2[k, b] = both(s1[k, one, b], r2[k, b]).astype(BF16)
        copies[3, k] = send(
            s2.at[k, 1 - two], r3.at[k], rs_send.at[2, k], rs_recv.at[2, k], device
        )
    input_back_group(2)
    for k in order:
        copies[3, k].wait_recv()
        two = y if k % 2 == 0 else x
        if k != 0:
            s3[k] = both(s2[k, two], r3[k]).astype(BF16)
            copies[4, k] = send(
                s3.at[k], r4.at[k], rs_send.at[3, k], rs_recv.at[3, k], z_dev(ahead(k))
            )
    grad = both(s2[0, y], r3[0])
    for k in (1, 3, 2):
        copies[4, k].wait_recv()
        grad = grad + r4[k].astype(F32)
    grad = grad[0:LINES, :]
    grad_out[...] = grad

    master_next, _, _ = adam(grad, master[...], mean[...], square[...])
    rows_in[0:LINES, :] = master_next
    taps = [rows_in[pl.ds(t, SHARD_ROWS, stride=9), :] for t in range(9)]
    plain, squares = taps[0], taps[0] * taps[0]
    for tap in taps[1:]:
        plain, squares = plain + tap, squares + tap * tap
    shape = (SHARD_ROWS, CG)
    first_chan = (dp * 2 + x) * SHARD_ROWS
    chan = lax.broadcasted_iota(jnp.int32, shape, 0) + first_chan
    lane = lax.broadcasted_iota(jnp.int32, shape, 1)
    picked = jnp.zeros(shape, F32)
    for g in range(GROUPS):
        picked += jnp.where(lane + g * CG == chan, gain[g : g + 1, :], 0.0)
    own_gain = jnp.sum(picked, axis=1, keepdims=True)
    chan_mean, chan_scale = channel_scale(
        jnp.sum(plain, axis=1, keepdims=True), jnp.sum(squares, axis=1, keepdims=True), own_gain
    )
    rows_out[104:SLOT, :] = jnp.zeros((8, CG), F32)
    for t in range(9):
        rows_out[pl.ds(t, SHARD_ROWS, stride=9), :] = (taps[t] - chan_mean) * chan_scale
    kb[z, c, y, x] = rows_out[...].astype(BF16)

    own_slot = kb.at[z, c, y, x]
    for k in (2, 1, 3):
        copies[5, k] = send(
            own_slot, own_slot, ag_send.at[0, k], ag_recv.at[0, k], z_dev(ahead(k))
        )
    order = (0, 1, 3, 2)
    for k in order:
        if k != 0:
            copies[5, k].wait_recv()
        slot = kb.at[behind(k), c, y, x]
        copies[6, k] = send(
            slot, slot, ag_send.at[1, k], ag_recv.at[1, k], x_dev if k % 2 == 0 else y_dev
        )
    for k in order:
        copies[6, k].wait_recv()
        zc = behind(k)
        slot = kb.at[zc, c, y] if k % 2 == 0 else kb.at[zc, c, :, x]
        copies[7, k] = send(
            slot, slot, ag_send.at[2, k], ag_recv.at[2, k], y_dev if k % 2 == 0 else x_dev
        )
    for k in order:
        copies[7, k].wait_recv()
        slot = kb.at[behind(k), c]
        copies[8, k] = send(slot, slot, ag_send.at[3, k], ag_recv.at[3, k], core_dev)
    for k in order:
        copies[8, k].wait_recv()
        zc = behind(k)
        for yc in range(2):
            for cc in range(2):
                for xc in range(2):
                    first = ((yc * 2 + cc) * 2 + xc) * LINES
                    kf[first : first + LINES, :] = kb[zc, cc, yc, xc].astype(F32)[0:LINES, :]
        rows = pl.ds(pl.multiple_of(zc * 96, 96), 96)
        for t in range(9):
            ker_out[rows, t * CG : t * CG + CG] = kf[pl.ds(t, 96, stride=9), :].astype(BF16)
    for copy in copies.values():
        copy.wait_send()


def fused_on_device(
    activations, cotangent, kernel, channel_gain, master_flat, moment_mean, moment_square
):
    vmem = pl.BlockSpec(memory_space=pltpu.VMEM)
    back, grad, kernel_next = pl.pallas_call(
        step_kernel,
        out_shape=(
            jax.ShapeDtypeStruct(activations.shape, BF16),
            jax.ShapeDtypeStruct((LINES, CG), F32),
            jax.ShapeDtypeStruct((CMID, FAN), BF16),
        ),
        in_specs=[vmem] * 7,
        out_specs=(vmem,) * 3,
        scratch_shapes=[
            pltpu.VMEM((2, 14, 16, CMID), F32),
            pltpu.VMEM((2, 14, 16, CMID), F32),
            pltpu.VMEM((2, 16, 16, 9 * CG), BF16),
            pltpu.VMEM((2, 16, 16, 9 * CG), BF16),
            pltpu.VMEM((3472, CG), F32),
            pltpu.VMEM((4, 2, 2, 2, SLOT, CG), BF16),
            pltpu.VMEM((4, 2, 2, SLOT, CG), BF16),
            pltpu.VMEM((4, 2, 2, SLOT, CG), BF16),
            pltpu.VMEM((4, 2, SLOT, CG), BF16),
            pltpu.VMEM((4, 2, SLOT, CG), BF16),
            pltpu.VMEM((4, SLOT, CG), BF16),
            pltpu.VMEM((4, SLOT, CG), BF16),
            pltpu.VMEM((4, SLOT, CG), BF16),
            pltpu.VMEM((4, 2, 2, 2, SLOT, CG), BF16),
            pltpu.VMEM((96 * 9, CG), F32),
            pltpu.VMEM((SLOT, CG), F32),
            pltpu.VMEM((SLOT, CG), F32),
            pltpu.SemaphoreType.DMA((4, 4)),
            pltpu.SemaphoreType.DMA((4, 4)),
            pltpu.SemaphoreType.DMA((4, 4)),
            pltpu.SemaphoreType.DMA((4, 4)),
        ],
        compiler_params=pltpu.CompilerParams(
            collective_id=0, has_side_effects=True, vmem_limit_bytes=40 * 1024 * 1024
        ),
        cost_estimate=pl.CostEstimate(
            flops=1_100_000_000, bytes_accessed=4_000_000, transcendentals=400_000
        ),
    )(
        activations, cotangent, kernel, channel_gain.reshape(GROUPS, CG),
        master_flat.reshape(LINES, CG), moment_mean.reshape(LINES, CG),
        moment_square.reshape(LINES, CG),
    )
    master_next, mean_next, square_next = adam(
        grad.reshape(-1), master_flat, moment_mean, moment_square
    )
    return (back, master_next, mean_next, square_next, kernel_next)


def solution(mesh):
    placed = (
        P(("dp", "sub"), None, None, None),
        P(("dp", "sub"), None, None, None),
        P(),
        P(),
        P(("dp", "sub")),
        P(("dp", "sub")),
        P(("dp", "sub")),
    )
    fused = dict(mesh.shape) == {"dp": 16, "sub": 2}
    return jax.shard_map(
        fused_on_device if fused else on_device,
        mesh=mesh,
        in_specs=placed,
        out_specs=(
            P(("dp", "sub"), None, None, None),
            P(("dp", "sub")),
            P(("dp", "sub")),
            P(("dp", "sub")),
            P(),
        ),
        check_vma=False,
    )
```
